128 devices in a mesh: gx: 8 (over y, core), gy: 16 (over x, z).
Axes of the slice: x: 4, y: 4, z: 4, core: 2. Of those that a mesh axis runs over, the one named last changes fastest.
Arguments:
- item_table: bfloat16 [2097152, 128], P(('gx', 'gy'))
- block_ids: int32 [16384, 8], P(('gx', 'gy')), may hold values from 0 to 262143, as said below
- item_slots: int32 [16384, 32], P(('gx', 'gy')), may hold values from 0 to 7
- item_offsets: int32 [16384, 32], P(('gx', 'gy')), may hold values from 0 to 7
- confidence: float32 [16384, 32], P(('gx', 'gy')), may hold values from 0.5 to 4
- item_counts: int32 [16384], P(('gx', 'gy')), may hold values from 8 to 32
- owner_map: int32 [262144], replicated, may hold values from 0 to 262143, as said below
Outputs:
- user_factors: float32 [16384, 128], P(('gx', 'gy'))
The draws below stay inside these ranges and needn't reach their ends.
Inputs may be any that keep to these rules, and one draw needn't show every extreme that they name: `block_ids`: each device's users (128 rows, 8 slots each) name at most 16 blocks b whose storage block owner_map[b] lies on any one device (owner_map[b] // 2048); one device holds exactly 16 of the named blocks of every device's users. `owner_map`: A permutation of the block numbers.
All inputs are finite; a program needn't handle non-finite values.
Results may differ from the reference program's by a relative error of at most 0.0014.
Values may be sent and summed in bfloat16 or wider, within the bound.
A program may use at most 64 MiB of HBM per device.

```python
import math
import jax
import jax.numpy as jnp
from jax import lax

LATENT = 128
BLOCK = 8
USER_BLOCKS = 8
USER_ITEMS = 32
ITERATIONS = 16
BLOCKS_DEV = 2048
USERS_DEV = 128
SHARDS = 128
ITEMS = 2097152
BLOCKS = 262144
USERS = 16384
CAPACITY = 16


def storage_order(key):
    return jax.random.permutation(jax.random.fold_in(key, 11), BLOCKS)


def draw_owner_map(key, part):
    return storage_order(key).astype(jnp.int32)


def draw_block_ids(key, part):
    ordering = storage_order(key)
    key = jax.random.fold_in(key, 5)
    key_busy, key_source = jax.random.split(key)
    busiest = jax.random.randint(key_busy, (), 0, SHARDS)
    slots_dev = USERS_DEV * USER_BLOCKS
    places = SHARDS * CAPACITY

    def one_source(key_one):
        key_shuffle, key_mixing, key_within = jax.random.split(key_one, 3)
        shuffled = jax.random.permutation(key_shuffle, places)
        owners = shuffled // CAPACITY
        ranking = jnp.where(owners == busiest, 0, 1 + jnp.arange(places))
        chosen = shuffled[jnp.argsort(ranking, stable=True)][:slots_dev]
        chosen = chosen[jax.random.permutation(key_mixing, slots_dev)]
        within = jax.random.randint(key_within, (slots_dev,), 0, BLOCKS_DEV)
        return chosen // CAPACITY * BLOCKS_DEV + within
    stored = jax.vmap(one_source)(jax.random.split(key_source, SHARDS))
    inverse = jnp.argsort(ordering, stable=True)
    return inverse[stored].reshape(USERS, USER_BLOCKS).astype(jnp.int32)


def draw_item_table(key, part):
    key = jax.random.fold_in(key, 3)
    key_column, key_base, key_rows = jax.random.split(key, 3)
    columns = jnp.exp(jax.random.uniform(key_column, (1, LATENT), jnp.float32, jnp.log(0.5), jnp.log(2.0)))
    rows = jnp.exp(jax.random.uniform(key_rows, (ITEMS, 1), jnp.float32, jnp.log(0.5), jnp.log(2.0)))
    rising = 1.0 + 2.0 * jnp.arange(ITEMS, dtype=jnp.float32)[:, None] / ITEMS
    base = jax.random.normal(key_base, (ITEMS, LATENT), jnp.float32)
    mixed = base + 0.5 * jnp.roll(base, 1, axis=1) + 0.5 * jnp.roll(base, 3, axis=1)
    return (mixed * columns * rows * rising * 0.04).astype(jnp.bfloat16)


def touch_ends(entries, key, low, top_value):
    place = [jax.random.randint(jax.random.fold_in(key, axis), (), 0, length) for axis, length in enumerate(entries.shape)]
    widest = entries.shape.index(max(entries.shape))
    beside = place[:widest] + [(place[widest] + 1) % entries.shape[widest]] + place[widest + 1:]
    return entries.at[tuple(place)].set(low).at[tuple(beside)].set(top_value)


def level_of(own_key, extent, cuts, least, high):
    factor_of, own = 1.0, jax.random.fold_in(own_key, 6)
    for axis_at, blocks in cuts:
        heights = jnp.exp(jax.random.uniform(jax.random.fold_in(own, axis_at), (blocks,), jnp.float32, least / len(cuts), high / len(cuts)))
        factor_of = factor_of * jnp.repeat(heights, extent[axis_at] // blocks).reshape([-1 if axis == axis_at else 1 for axis in range(len(extent))])
    return factor_of


def setup_inputs(seed: int = 0) -> dict:
    streams_of = jax.random.split(jax.random.key(seed), 8)
    item_table = draw_item_table(jax.random.fold_in(streams_of[7], 71), 0)
    block_ids = draw_block_ids(jax.random.fold_in(streams_of[7], 71), 0)
    item_slots = touch_ends(jax.random.randint(streams_of[2], (USERS, USER_ITEMS), 0, USER_BLOCKS), jax.random.fold_in(streams_of[2], 1), 0, USER_BLOCKS - 1).astype(jnp.int32)
    item_offsets = touch_ends(jax.random.randint(streams_of[3], (USERS, USER_ITEMS), 0, BLOCK), jax.random.fold_in(streams_of[3], 1), 0, BLOCK - 1).astype(jnp.int32)
    confidence = jnp.clip(jnp.exp(math.log(4.0) - 2.0794415 * jax.random.uniform(streams_of[4], (USERS, USER_ITEMS), jnp.float32) ** level_of(streams_of[4], (USERS, USER_ITEMS), ((0, 128),), -0.2, 0.2)), 0.5, 4.0)
    item_counts = touch_ends(jax.random.randint(streams_of[5], (USERS,), USER_ITEMS // 4, USER_ITEMS + 1), jax.random.fold_in(streams_of[5], 1), USER_ITEMS // 4, USER_ITEMS).astype(jnp.int32)
    owner_map = draw_owner_map(jax.random.fold_in(streams_of[7], 71), 0)
    return {"item_table": item_table, "block_ids": block_ids, "item_slots": item_slots, "item_offsets": item_offsets, "confidence": confidence, "item_counts": item_counts, "owner_map": owner_map}


REGULAR = 1.0


def apply_normal(direction, gramian, vectors, weights, unobserved):
    highest = lax.Precision.HIGHEST
    projected = jnp.einsum("ulk,uk->ul", vectors, direction, precision=highest)
    returned = jnp.einsum("ulk,ul->uk", vectors, weights * projected, precision=highest)
    return unobserved * jnp.dot(direction, gramian, precision=highest) + returned + REGULAR * direction


def conjugate(gramian, vectors, weights, unobserved):
    highest = lax.Precision.HIGHEST
    right_side = jnp.einsum("ul,ulk->uk", weights, vectors, precision=highest)
    solution = jnp.zeros_like(right_side)
    norm_now = jnp.sum(right_side * right_side, axis=1, keepdims=True)

    def sweep(index_now, carry):
        solution, residual, direction, norm_now = carry
        image = apply_normal(direction, gramian, vectors, weights, unobserved)
        alpha = norm_now / jnp.sum(direction * image, axis=1, keepdims=True)
        solution = solution + alpha * direction
        residual = residual - alpha * image
        norm_next = jnp.sum(residual * residual, axis=1, keepdims=True)
        direction = residual + (norm_next / norm_now) * direction
        return (solution, residual, direction, norm_next)

    result = lax.fori_loop(0, ITERATIONS, sweep, (solution, right_side, right_side, norm_now))
    return result[0]


def reference(item_table, block_ids, item_slots, item_offsets, confidence, item_counts, owner_map):
    gramian = lax.dot_general(item_table, item_table, (((0,), (0,)), ((), ())), preferred_element_type=jnp.float32)
    unobserved = USER_ITEMS / ITEMS
    live = jnp.arange(USER_ITEMS)[None, :] < item_counts[:, None]
    weights = jnp.where(live, confidence, 0.0).astype(jnp.float32)
    storage = owner_map[block_ids].astype(jnp.int32)
    row_index = (jnp.take_along_axis(storage, item_slots, axis=1) * BLOCK + item_offsets).astype(jnp.int32)
    groups = USERS // USERS_DEV

    def solve_group(packed):
        index_group, weight_group = packed
        vectors = item_table[index_group].astype(jnp.float32)
        return conjugate(gramian, vectors, weight_group, unobserved)

    solved = lax.map(solve_group, (row_index.reshape(groups, USERS_DEV, USER_ITEMS), weights.reshape(groups, USERS_DEV, USER_ITEMS)))
    return solved.reshape(USERS, LATENT)
```

```python
import functools

import jax
import jax.numpy as jnp
from jax import lax
from jax.experimental import pallas as pl
from jax.experimental.pallas import tpu as pltpu
from jax.sharding import PartitionSpec as P

BLOCK = 8
USER_BLOCKS = 8
USER_ITEMS = 32
ITERATIONS = 16
LANES = 128
ROOM = 64
MOST = 128
MARK = 1 << 20

MESH = pl.DeviceIdType.MESH
F32 = jnp.float32
BF16 = jnp.bfloat16
VMEM_LIMIT = 56 * 1024 * 1024


def place(gy_size):
    gx, gy = lax.axis_index("gx"), lax.axis_index("gy")
    return gx * gy_size + gy


def signal_all(me, shards, gy_size):
    barrier = pltpu.get_barrier_semaphore()

    def one(i, carry):
        peer = lax.rem(me + i, shards)
        pl.semaphore_signal(
            barrier,
            inc=1,
            device_id=(peer // gy_size, lax.rem(peer, gy_size)),
            device_id_type=MESH,
        )
        return carry

    lax.fori_loop(1, shards, one, 0)
    return barrier


def send(src, dst, send_sem, recv_sem, peer, gy_size):
    return pltpu.make_async_remote_copy(
        src_ref=src,
        dst_ref=dst,
        send_sem=send_sem,
        recv_sem=recv_sem,
        device_id=(peer // gy_size, lax.rem(peer, gy_size)),
        device_id_type=MESH,
    )


def exchange_rows(table, landing, me, shards, gy_size, send_sem, recv_sem):
    def one(i, carry):
        peer = lax.rem(me + i, shards)
        send(table.at[peer], landing.at[me], send_sem, recv_sem, peer, gy_size).start()
        return carry

    lax.fori_loop(1, shards, one, 0)


def await_rows(table, landing, shards, gy_size, send_sem, recv_sem):
    others = pl.ds(0, shards - 1)
    send(table.at[others], landing.at[others], send_sem, recv_sem, 0, gy_size).wait()


def ask_kernel(
    shards, gy_size, blocks_dev, ids, owner_map, need, asked, keys, top,
    owners, found, queries, map_sem, own_sem, send_sem, recv_sem,
):
    me = place(gy_size)
    barrier = signal_all(me, shards, gy_size)
    load = pltpu.make_async_copy(owner_map, owners, map_sem)
    load.start()
    requests = found.shape[0]
    lane_row = lax.broadcasted_iota(jnp.int32, (1, LANES), 1)
    load.wait()

    def look(j, carry):
        for t in range(8):
            i = j * 8 + t
            block = ids[i // LANES, lax.rem(i, LANES)]
            row = owners[pl.ds(lax.shift_right_logical(block, 7), 1), :]
            found[pl.ds(i, 1), :] = jnp.where(lane_row == (block & (LANES - 1)), row, 0)
        return carry

    lax.fori_loop(0, requests // 8, look, 0)

    chunk = LANES
    lane = lax.broadcasted_iota(jnp.int32, (chunk, LANES), 1)
    sub = lax.broadcasted_iota(jnp.int32, (chunk, LANES), 0)
    lane8 = lax.broadcasted_iota(jnp.int32, (chunk, BLOCK), 1)
    earlier = jnp.where(lane < sub, 1.0, 0.0).astype(BF16)
    total = jnp.zeros((1, LANES), F32)
    low = jnp.zeros((LANES, LANES), F32)
    high = jnp.zeros((LANES, LANES), F32)
    over_rows = (((0,), (0,)), ((), ()))
    for a in range(requests // chunk):
        rows = pl.ds(a * chunk, chunk)
        storage = jnp.sum(found[rows, :].astype(F32), axis=1, keepdims=True).astype(jnp.int32)
        owner = storage // blocks_dev
        within = storage - owner * blocks_dev
        wanted = need[rows, :]
        count = jnp.sum(wanted, axis=1, keepdims=True)
        mine = owner == lane
        one_hot = jnp.where(mine, 1.0, 0.0).astype(BF16)
        counted = jnp.where(mine, count, 0.0)
        before = jnp.dot(earlier, counted.astype(BF16), preferred_element_type=F32) + total
        start = jnp.sum(jnp.where(mine, before, 0.0), axis=1, keepdims=True).astype(jnp.int32)
        total = total + jnp.sum(counted, axis=0, keepdims=True)
        first = within * BLOCK
        low_here = jnp.zeros((chunk, LANES), F32)
        high_here = jnp.zeros((chunk, LANES), F32)
        key = jnp.zeros((chunk, BLOCK), jnp.int32)
        for r in range(BLOCK):
            live = wanted[:, r : r + 1]
            row = first + r
            hit = jnp.where(lane == start, live, 0.0)
            low_here = low_here + hit * (row & (LANES - 1)).astype(F32)
            high_here = high_here + hit * lax.shift_right_logical(row, 7).astype(F32)
            spot = jnp.where(live > 0.0, owner * MOST + start, 0)
            key = jnp.where(lane8 == r, spot, key)
            start = start + live.astype(jnp.int32)
        keys[rows, :] = key
        low = low + lax.dot_general(
            one_hot, low_here.astype(BF16), over_rows, preferred_element_type=F32
        )
        high = high + lax.dot_general(
            one_hot, high_here.astype(BF16), over_rows, preferred_element_type=F32
        )
    most = jnp.max(total, axis=1, keepdims=True)
    mark = jnp.where(most > ROOM, float(MARK), 0.0)
    query = (low + high * float(LANES) + mark).astype(jnp.int32)
    for o in range(shards):
        queries[o] = query[o : o + 1, :]

    pl.semaphore_wait(barrier, shards - 1)
    exchange_rows(queries, asked, me, shards, gy_size, send_sem, recv_sem)
    own = pltpu.make_async_copy(queries.at[me], asked.at[me], own_sem)
    own.start()
    own.wait()
    await_rows(queries, asked, shards, gy_size, send_sem, recv_sem)
    top[...] = jnp.max(jnp.max(asked[...], axis=0), axis=1, keepdims=True)


def fetch_kernel(
    shards, gy_size, room, asked, table, landed, gramian,
    packed, wide, stage, outgoing, terms, arrived, row_total, table_sem, own_sem,
    send_sem, recv_sem, term_send, term_recv, sum_send, sum_recv,
):
    me = place(gy_size)
    barrier = signal_all(me, shards, gy_size)
    rows_dev = table.shape[0]
    parts = 8
    part = rows_dev // parts

    def load(c):
        rows = pl.ds(c * part, part)
        return pltpu.make_async_copy(table.at[rows], packed.at[rows], table_sem.at[c])

    for c in range(parts):
        load(c).start()
    piece = min(512, part)
    total = jnp.zeros((LANES, LANES), F32)
    for c in range(parts):
        load(c).wait()

        def step(j, total):
            rows = pl.ds(pl.multiple_of(c * part + j * piece, piece), piece)
            block = packed[rows, :]
            wide[rows, :] = block.astype(F32)
            return total + lax.dot_general(
                block, block, (((0,), (0,)), ((), ())), preferred_element_type=F32
            )

        total = lax.fori_loop(0, part // piece, step, total)
    for o in range(shards):
        terms[o] = total[o : o + 1, :]

    pl.semaphore_wait(barrier, shards - 1)
    exchange_rows(terms, arrived, me, shards, gy_size, term_send, term_recv)
    own_term = pltpu.make_async_copy(terms.at[me], arrived.at[me], own_sem.at[0])
    own_term.start()

    def collect(peer):
        for h in range(room // 16):
            for t in range(16):
                row = asked[peer, h * 16 + t] & (MARK - 1)
                stage[pl.ds(h * 16 + t, 1), :] = wide[pl.ds(row, 1), :]
        outgoing[peer] = stage[...].astype(BF16)

    def serve(i, carry):
        off = lax.rem(i * 37, shards)
        peer = lax.rem(me + off, shards)
        collect(peer)
        send(outgoing.at[peer], landed.at[me], send_sem, recv_sem, peer, gy_size).start()
        return carry

    lax.fori_loop(1, shards // 2, serve, 0)
    own_term.wait()
    await_rows(terms, arrived, shards, gy_size, term_send, term_recv)
    row_total[...] = jnp.sum(arrived[...], axis=0)

    def share(i, carry):
        peer = lax.rem(me + i, shards)
        send(row_total, gramian.at[me], sum_send, sum_recv, peer, gy_size).start()
        return carry

    lax.fori_loop(1, shards, share, 0)
    own_sum = pltpu.make_async_copy(row_total, gramian.at[me], own_sem.at[1])
    own_sum.start()
    lax.fori_loop(shards // 2, shards, serve, 0)
    collect(me)
    own = pltpu.make_async_copy(outgoing.at[me], landed.at[me], own_sem.at[2])
    own.start()
    own_sum.wait()
    own.wait()
    await_rows(terms, gramian, shards, gy_size, sum_send, sum_recv)
    await_rows(outgoing, landed, shards, gy_size, send_sem, recv_sem)


def solve_kernel(unobserved, spots, landed, gramian, weights, out, packed, wide, vectors, sem):
    users = weights.shape[1]
    rows = landed.shape[0]
    parts = 8
    part = rows // parts

    def load(c):
        here = pl.ds(c * part, part)
        return pltpu.make_async_copy(landed.at[here], packed.at[here], sem.at[c])

    for c in range(parts):
        load(c).start()
    for c in range(parts):
        load(c).wait()
        here = pl.ds(c * part, part)
        wide[here, :] = packed[here, :].astype(F32)

    def pick(item, carry):
        def some(j, carry):
            for t in range(16):
                user = j * 16 + t
                spot = spots[item, user]
                vectors[item, pl.ds(user, 1), :] = wide[pl.ds(spot, 1), :]
            return carry

        lax.fori_loop(0, users // 16, some, 0)
        vectors[item] = vectors[item].T
        return carry

    lax.fori_loop(0, USER_ITEMS, pick, 0)

    scaled = gramian[...] * unobserved
    top = scaled.astype(BF16)
    rest = (scaled - top.astype(F32)).astype(BF16)

    right = jnp.zeros((LANES, users), F32)
    for item in range(USER_ITEMS):
        right = right + vectors[item] * weights[item : item + 1, :]
    norm = jnp.sum(right * right, axis=0, keepdims=True)

    def sweep(_, carry):
        solution, residual, direction, norm = carry
        d_top = direction.astype(BF16)
        d_rest = (direction - d_top.astype(F32)).astype(BF16)
        image = direction + (
            jnp.dot(top, d_top, preferred_element_type=F32)
            + jnp.dot(top, d_rest, preferred_element_type=F32)
            + jnp.dot(rest, d_top, preferred_element_type=F32)
        )
        for item in range(USER_ITEMS):
            vector = vectors[item]
            projected = jnp.sum(vector * direction, axis=0, keepdims=True)
            image = image + vector * (weights[item : item + 1, :] * projected)
        alpha = norm / jnp.sum(direction * image, axis=0, keepdims=True)
        solution = solution + alpha * direction
        residual = residual - alpha * image
        after = jnp.sum(residual * residual, axis=0, keepdims=True)
        direction = residual + (after / norm) * direction
        return solution, residual, direction, after

    solution, *_ = lax.fori_loop(
        0, ITERATIONS, sweep, (jnp.zeros_like(right), right, right, norm)
    )
    out[...] = solution.T


def vmem():
    return pl.BlockSpec(memory_space=pltpu.VMEM)


def smem():
    return pl.BlockSpec(memory_space=pltpu.SMEM)


def anywhere():
    return pl.BlockSpec(memory_space=pl.ANY)


def ask(shards, gy_size, blocks_dev, ids, owner_map, need):
    requests = need.shape[0]
    dma = pltpu.SemaphoreType.DMA
    return pl.pallas_call(
        functools.partial(ask_kernel, shards, gy_size, blocks_dev),
        out_shape=(
            jax.ShapeDtypeStruct((shards, 1, LANES), jnp.int32),
            jax.ShapeDtypeStruct((requests, BLOCK), jnp.int32),
            jax.ShapeDtypeStruct((1, 1), jnp.int32),
        ),
        in_specs=[smem(), anywhere(), vmem()],
        out_specs=(vmem(), vmem(), vmem()),
        scratch_shapes=[
            pltpu.VMEM(owner_map.shape, jnp.int32),
            pltpu.VMEM((requests, LANES), jnp.int32),
            pltpu.VMEM((shards, 1, LANES), jnp.int32),
            dma, dma, dma, dma,
        ],
        compiler_params=pltpu.CompilerParams(
            collective_id=0, has_side_effects=True, vmem_limit_bytes=VMEM_LIMIT
        ),
        name="ask",
    )(ids, owner_map, need)


def fetch(shards, gy_size, room, asked, table):
    dma = pltpu.SemaphoreType.DMA
    return pl.pallas_call(
        functools.partial(fetch_kernel, shards, gy_size, room),
        out_shape=(
            jax.ShapeDtypeStruct((shards, room, LANES), BF16),
            jax.ShapeDtypeStruct((shards, 1, LANES), F32),
        ),
        in_specs=[smem(), anywhere()],
        out_specs=(anywhere(), vmem()),
        scratch_shapes=[
            pltpu.VMEM(table.shape, BF16),
            pltpu.VMEM(table.shape, F32),
            pltpu.VMEM((room, LANES), F32),
            pltpu.VMEM((shards, room, LANES), BF16),
            pltpu.VMEM((shards, 1, LANES), F32),
            pltpu.VMEM((shards, 1, LANES), F32),
            pltpu.VMEM((1, LANES), F32),
            pltpu.SemaphoreType.DMA((8,)),
            pltpu.SemaphoreType.DMA((3,)),
            dma, dma, dma, dma, dma, dma,
        ],
        compiler_params=pltpu.CompilerParams(
            collective_id=1 if room == ROOM else 2,
            has_side_effects=True,
            vmem_limit_bytes=VMEM_LIMIT,
        ),
        name="fetch",
    )(asked, table)


def solve(unobserved, spots, landed, gramian, weights):
    users = weights.shape[1]
    return pl.pallas_call(
        functools.partial(solve_kernel, unobserved),
        out_shape=jax.ShapeDtypeStruct((users, LANES), F32),
        in_specs=[smem(), anywhere(), vmem(), vmem()],
        out_specs=vmem(),
        scratch_shapes=[
            pltpu.VMEM(landed.shape, BF16),
            pltpu.VMEM(landed.shape, F32),
            pltpu.VMEM((USER_ITEMS, users, LANES), F32),
            pltpu.SemaphoreType.DMA((8,)),
        ],
        compiler_params=pltpu.CompilerParams(vmem_limit_bytes=VMEM_LIMIT),
        name="solve",
    )(spots, landed, gramian, weights)


def per_device(item_table, block_ids, item_slots, item_offsets, confidence, item_counts, owner_map):
    shards, gy_size = lax.axis_size(("gx", "gy")), lax.axis_size("gy")
    rows_dev = item_table.shape[0]
    blocks_dev = rows_dev // BLOCK
    users = block_ids.shape[0]
    unobserved = USER_ITEMS / (rows_dev * shards)

    live = jnp.arange(USER_ITEMS)[None, :] < item_counts[:, None]
    weights = jnp.where(live, confidence, 0.0).T
    row_index = item_slots * BLOCK + item_offsets
    candidates = jnp.arange(USER_BLOCKS * BLOCK, dtype=jnp.int32)
    hits = (row_index[:, :, None] == candidates[None, None, :]) & live[:, :, None]
    need = jnp.any(hits, axis=1).astype(F32).reshape(users * USER_BLOCKS, BLOCK)

    asked, keys, top = ask(
        shards,
        gy_size,
        blocks_dev,
        block_ids.reshape(-1, LANES),
        owner_map.reshape(-1, LANES),
        need,
    )
    asked = asked.reshape(shards, LANES)
    keys = keys.reshape(users, USER_BLOCKS * BLOCK)
    key = jnp.sum(
        jnp.where(row_index.T[:, :, None] == candidates[None, None, :], keys[None, :, :], 0),
        axis=2,
    )

    def finish(room):
        def branch(asked, key, weights, item_table):
            landed, gramian = fetch(shards, gy_size, room, asked, item_table)
            spots = (key // MOST) * room + lax.rem(key, MOST)
            landed = landed.reshape(shards * room, LANES)
            return solve(unobserved, spots, landed, gramian.reshape(LANES, LANES), weights)

        return branch

    return lax.cond(
        top[0, 0] >= MARK, finish(MOST), finish(ROOM), asked, key, weights, item_table
    )


def solution(mesh):
    return jax.shard_map(
        per_device,
        mesh=mesh,
        in_specs=(
            P(("gx", "gy"), None),
            P(("gx", "gy"), None),
            P(("gx", "gy"), None),
            P(("gx", "gy"), None),
            P(("gx", "gy"), None),
            P(("gx", "gy")),
            P(),
        ),
        out_specs=P(("gx", "gy"), None),
        check_vma=False,
    )
```

```python
import functools

import jax
import jax.numpy as jnp
from jax import lax
from jax.experimental import pallas as pl
from jax.experimental.pallas import tpu as pltpu
from jax.sharding import PartitionSpec as P

BLOCK = 8
USER_BLOCKS = 8
USER_ITEMS = 32
ITERATIONS = 16
LANES = 128
CORES = 2
RING = 4
ROOM = 48
CHIP_ROOM = CORES * ROOM
MOST = 128
MARK = 1 << 20

MESH = pl.DeviceIdType.MESH
F32 = jnp.float32
BF16 = jnp.bfloat16
VMEM_LIMIT = 56 * 1024 * 1024


def place(gy_size):
    gx, gy = lax.axis_index("gx"), lax.axis_index("gy")
    return gx * gy_size + gy


def signal_all(me, shards, gy_size):
    barrier = pltpu.get_barrier_semaphore()

    def one(i, carry):
        peer = lax.rem(me + i, shards)
        pl.semaphore_signal(
            barrier,
            inc=1,
            device_id=(peer // gy_size, lax.rem(peer, gy_size)),
            device_id_type=MESH,
        )
        return carry

    lax.fori_loop(1, shards, one, 0)
    return barrier


def send(src, dst, send_sem, recv_sem, peer, gy_size):
    return pltpu.make_async_remote_copy(
        src_ref=src,
        dst_ref=dst,
        send_sem=send_sem,
        recv_sem=recv_sem,
        device_id=(peer // gy_size, lax.rem(peer, gy_size)),
        device_id_type=MESH,
    )


def exchange_rows(table, landing, me, shards, gy_size, send_sem, recv_sem):
    def one(i, carry):
        peer = lax.rem(me + i, shards)
        send(table.at[peer], landing.at[me], send_sem, recv_sem, peer, gy_size).start()
        return carry

    lax.fori_loop(1, shards, one, 0)


def await_rows(table, landing, shards, gy_size, send_sem, recv_sem):
    others = pl.ds(0, shards - 1)
    send(table.at[others], landing.at[others], send_sem, recv_sem, 0, gy_size).wait()


def ask_kernel(
    shards, gy_size, blocks_dev, ids, owner_map, need, asked, keys, top,
    owners, found, queries, map_sem, own_sem, send_sem, recv_sem,
):
    me = place(gy_size)
    barrier = signal_all(me, shards, gy_size)
    load = pltpu.make_async_copy(owner_map, owners, map_sem)
    load.start()
    requests = found.shape[0]
    lane_row = lax.broadcasted_iota(jnp.int32, (1, LANES), 1)
    load.wait()

    def look(j, carry):
        for t in range(8):
            i = j * 8 + t
            block = ids[i // LANES, lax.rem(i, LANES)]
            row = owners[pl.ds(lax.shift_right_logical(block, 7), 1), :]
            found[pl.ds(i, 1), :] = jnp.where(lane_row == (block & (LANES - 1)), row, 0)
        return carry

    lax.fori_loop(0, requests // 8, look, 0)

    chunk = LANES
    lane = lax.broadcasted_iota(jnp.int32, (chunk, LANES), 1)
    sub = lax.broadcasted_iota(jnp.int32, (chunk, LANES), 0)
    lane8 = lax.broadcasted_iota(jnp.int32, (chunk, BLOCK), 1)
    earlier = jnp.where(lane < sub, 1.0, 0.0).astype(BF16)
    total = jnp.zeros((1, LANES), F32)
    low = jnp.zeros((LANES, LANES), F32)
    high = jnp.zeros((LANES, LANES), F32)
    over_rows = (((0,), (0,)), ((), ()))
    for a in range(requests // chunk):
        rows = pl.ds(a * chunk, chunk)
        storage = jnp.sum(found[rows, :].astype(F32), axis=1, keepdims=True).astype(jnp.int32)
        owner = storage // blocks_dev
        within = storage - owner * blocks_dev
        wanted = need[rows, :]
        count = jnp.sum(wanted, axis=1, keepdims=True)
        mine = owner == lane
        one_hot = jnp.where(mine, 1.0, 0.0).astype(BF16)
        counted = jnp.where(mine, count, 0.0)
        before = jnp.dot(earlier, counted.astype(BF16), preferred_element_type=F32) + total
        start = jnp.sum(jnp.where(mine, before, 0.0), axis=1, keepdims=True).astype(jnp.int32)
        total = total + jnp.sum(counted, axis=0, keepdims=True)
        first = within * BLOCK
        low_here = jnp.zeros((chunk, LANES), F32)
        high_here = jnp.zeros((chunk, LANES), F32)
        key = jnp.zeros((chunk, BLOCK), jnp.int32)
        for r in range(BLOCK):
            live = wanted[:, r : r + 1]
            row = first + r
            hit = jnp.where(lane == start, live, 0.0)
            low_here = low_here + hit * (row & (LANES - 1)).astype(F32)
            high_here = high_here + hit * lax.shift_right_logical(row, 7).astype(F32)
            spot = jnp.where(live > 0.0, owner * MOST + start, 0)
            key = jnp.where(lane8 == r, spot, key)
            start = start + live.astype(jnp.int32)
        keys[rows, :] = key
        low = low + lax.dot_general(
            one_hot, low_here.astype(BF16), over_rows, preferred_element_type=F32
        )
        high = high + lax.dot_general(
            one_hot, high_here.astype(BF16), over_rows, preferred_element_type=F32
        )
    most = jnp.max(total, axis=1, keepdims=True)
    mark = jnp.where(most > MOST, float(MARK), 0.0)
    query = (low + high * float(LANES) + mark).astype(jnp.int32)
    for o in range(shards):
        queries[o] = query[o : o + 1, :]

    pl.semaphore_wait(barrier, shards - 1)
    exchange_rows(queries, asked, me, shards, gy_size, send_sem, recv_sem)
    own = pltpu.make_async_copy(queries.at[me], asked.at[me], own_sem)
    own.start()
    own.wait()
    await_rows(queries, asked, shards, gy_size, send_sem, recv_sem)
    top[...] = jnp.max(jnp.max(asked[...], axis=0), axis=1, keepdims=True)


def fetch_kernel(
    shards, gy_size, room, asked, table, landed, gramian,
    packed, wide, stage, outgoing, terms, arrived, row_total, table_sem, own_sem,
    send_sem, recv_sem, term_send, term_recv, sum_send, sum_recv,
):
    me = place(gy_size)
    barrier = signal_all(me, shards, gy_size)
    rows_dev = table.shape[0]
    parts = 8
    part = rows_dev // parts

    def load(c):
        rows = pl.ds(c * part, part)
        return pltpu.make_async_copy(table.at[rows], packed.at[rows], table_sem.at[c])

    for c in range(parts):
        load(c).start()
    piece = min(512, part)
    total = jnp.zeros((LANES, LANES), F32)
    for c in range(parts):
        load(c).wait()

        def step(j, total):
            rows = pl.ds(pl.multiple_of(c * part + j * piece, piece), piece)
            block = packed[rows, :]
            wide[rows, :] = block.astype(F32)
            return total + lax.dot_general(
                block, block, (((0,), (0,)), ((), ())), preferred_element_type=F32
            )

        total = lax.fori_loop(0, part // piece, step, total)
    for o in range(shards):
        terms[o] = total[o : o + 1, :]

    pl.semaphore_wait(barrier, shards - 1)
    exchange_rows(terms, arrived, me, shards, gy_size, term_send, term_recv)
    own_term = pltpu.make_async_copy(terms.at[me], arrived.at[me], own_sem.at[0])
    own_term.start()

    def collect(peer):
        for h in range(room // 16):
            for t in range(16):
                row = asked[peer, h * 16 + t] & (rows_dev - 1)
                stage[pl.ds(h * 16 + t, 1), :] = wide[pl.ds(row, 1), :]
        outgoing[peer] = stage[...].astype(BF16)

    def serve(i, carry):
        off = lax.rem(i * 37, shards)
        peer = lax.rem(me + off, shards)
        collect(peer)
        send(outgoing.at[peer], landed.at[me], send_sem, recv_sem, peer, gy_size).start()
        return carry

    lax.fori_loop(1, shards // 2, serve, 0)
    own_term.wait()
    await_rows(terms, arrived, shards, gy_size, term_send, term_recv)
    row_total[...] = jnp.sum(arrived[...], axis=0)

    def share(i, carry):
        peer = lax.rem(me + i, shards)
        send(row_total, gramian.at[me], sum_send, sum_recv, peer, gy_size).start()
        return carry

    lax.fori_loop(1, shards, share, 0)
    own_sum = pltpu.make_async_copy(row_total, gramian.at[me], own_sem.at[1])
    own_sum.start()
    lax.fori_loop(shards // 2, shards, serve, 0)
    collect(me)
    own = pltpu.make_async_copy(outgoing.at[me], landed.at[me], own_sem.at[2])
    own.start()
    own_sum.wait()
    own.wait()
    await_rows(terms, gramian, shards, gy_size, sum_send, sum_recv)
    await_rows(outgoing, landed, shards, gy_size, send_sem, recv_sem)


def bits(count):
    assert count & (count - 1) == 0
    return count.bit_length() - 1


def chip_of(device, gy_size):
    gx, gy = device // gy_size, lax.rem(device, gy_size)
    return (gx // CORES) * gy_size + gy, lax.rem(gx, CORES)


def shifted(me, off, gy_size):
    gx, gy = me // gy_size, lax.rem(me, gy_size)
    y, core, x, z = gx // CORES, lax.rem(gx, CORES), gy // RING, lax.rem(gy, RING)
    z = lax.rem(z + lax.rem(off, RING), RING)
    x = lax.rem(x + lax.rem(off // RING, RING), RING)
    core = lax.rem(core + lax.rem(off // (RING * RING), CORES), CORES)
    y = lax.rem(y + off // (RING * RING * CORES), RING)
    return (y * CORES + core) * gy_size + x * RING + z


def gather_kernel(
    shards, gy_size, blocks_dev, ids, id_rows, owner_map, slots, offsets, counts, table,
    landed, gramian, spots, top,
    owners, found, queries, asked, asked_here, packed, twin_packed, wide, stage, outgoing,
    terms, arrived, row_total, load_sem, own_sem, table_send, table_recv,
    send_sem, recv_sem, ask_send, ask_recv, term_send, term_recv, sum_send, sum_recv,
):
    me = place(gy_size)
    chip_me, core_me = chip_of(me, gy_size)
    barrier = signal_all(me, shards, gy_size)
    load_map = pltpu.make_async_copy(owner_map, owners, own_sem.at[0])
    load_map.start()
    rows_dev = table.shape[0]
    parts = 8
    part = rows_dev // parts

    def load(c):
        rows = pl.ds(c * part, part)
        return pltpu.make_async_copy(table.at[rows], packed.at[rows], load_sem.at[c])

    for c in range(parts):
        load(c).start()

    users = slots.shape[0]
    requests = found.shape[0]
    group = LANES // USER_BLOCKS
    lane = lax.broadcasted_iota(jnp.int32, (LANES, LANES), 1)
    sub = lax.broadcasted_iota(jnp.int32, (LANES, LANES), 0)
    lane_f = lane.astype(F32)
    diagonal = lane == sub

    count = jnp.sum(jnp.where(diagonal, counts[...], 0).astype(F32), axis=1, keepdims=True)
    slot_lane = lax.broadcasted_iota(jnp.int32, (users, USER_ITEMS), 1)
    row_index = slots[...] * BLOCK + offsets[...]
    row_index = jnp.where(slot_lane < count.astype(jnp.int32), row_index, -1)
    wanted = lane == row_index[:, 0:1]
    for item in range(1, USER_ITEMS):
        wanted = wanted | (lane == row_index[:, item : item + 1])
    wanted = jnp.where(wanted, 1.0, 0.0).astype(BF16)
    inner = jnp.zeros((users, LANES), F32)
    for slot in range(USER_BLOCKS):
        id_low = (id_rows[:, slot : slot + 1] & (LANES - 1)).astype(F32)
        inner = jnp.where(lane == slot, id_low, inner)
    inner = inner.astype(BF16)

    load_map.wait()

    def look(user, carry):
        for slot in range(USER_BLOCKS):
            line = lax.shift_right_logical(ids[user, slot], bits(LANES))
            found[pl.ds(user * USER_BLOCKS + slot, 1), :] = owners[pl.ds(line, 1), :]
        return carry

    lax.fori_loop(0, users, look, 0, unroll=2)

    same = lax.shift_right_logical(lane, 3) == (sub & 7)
    own_lane = lane == (sub & 7)
    earlier = jnp.where(lane < sub, 1.0, 0.0).astype(BF16)
    before_row = jnp.where(
        (lax.shift_right_logical(lane, 3) == lax.shift_right_logical(sub, 3))
        & ((sub & 7) < (lane & 7)),
        1.0,
        0.0,
    ).astype(BF16)
    up_to = [jnp.where((sub & 7) <= r, 1.0, 0.0).astype(BF16) for r in range(BLOCK)]
    total = jnp.zeros((1, LANES), F32)
    low_high = jnp.zeros((LANES, 2 * LANES), F32)
    pos_chip = jnp.zeros((users, 2 * LANES), F32)
    for a in range(requests // LANES):
        pick = jnp.where(sub // USER_BLOCKS + a * group == lane, 1.0, 0.0).astype(BF16)
        place_back = jnp.where(lane // USER_BLOCKS + a * group == sub, 1.0, 0.0).astype(BF16)
        spread = jnp.dot(pick, wanted, preferred_element_type=F32)
        spread = jnp.where(same, spread, 0.0)
        live = spread > 0.0
        spread = spread.astype(BF16)
        inner_here = jnp.dot(pick, inner, preferred_element_type=F32)
        inner_here = jnp.sum(jnp.where(own_lane, inner_here, 0.0), axis=1, keepdims=True)
        line = found[pl.ds(a * LANES, LANES), :].astype(F32)
        storage = jnp.sum(jnp.where(lane_f == inner_here, line, 0.0), axis=1, keepdims=True)
        storage = storage.astype(jnp.int32)
        device = lax.shift_right_logical(storage, bits(blocks_dev))
        within = storage & (blocks_dev - 1)
        gx = lax.shift_right_logical(device, bits(gy_size))
        chip = lax.shift_right_logical(gx, bits(CORES)) * gy_size + (device & (gy_size - 1))
        core = gx & (CORES - 1)
        low_first = ((within & 15) * BLOCK).astype(F32)
        high = (core * (rows_dev // LANES) + lax.shift_right_logical(within, 4)).astype(F32)
        chip = chip.astype(F32)
        so_far = [jnp.dot(spread, m, preferred_element_type=F32) for m in up_to]
        mine = lane_f == chip
        counted = jnp.where(mine, so_far[-1], 0.0)
        before = jnp.dot(earlier, counted.astype(BF16), preferred_element_type=F32) + total
        start = jnp.sum(jnp.where(mine, before, 0.0), axis=1, keepdims=True)
        total = total + jnp.sum(counted, axis=0, keepdims=True)
        depth = lane_f - start
        which = jnp.zeros((LANES, LANES), F32)
        for m in so_far:
            which = which + jnp.where(m <= depth, 1.0, 0.0)
        hit = (depth >= 0.0) & (depth < so_far[-1])
        both = jnp.concatenate(
            [jnp.where(hit, low_first + which, 0.0), jnp.where(hit, high, 0.0)], axis=1
        ).astype(BF16)
        chip_row = jnp.sum(jnp.where(diagonal, chip, 0.0), axis=0, keepdims=True)
        to_chip = jnp.where(sub.astype(F32) == chip_row, 1.0, 0.0).astype(BF16)
        low_high = low_high + jnp.dot(to_chip, both, preferred_element_type=F32)
        spot = jnp.dot(spread, before_row, preferred_element_type=F32) + start
        both = jnp.concatenate(
            [jnp.where(live, spot, 0.0), jnp.where(live, chip, 0.0)], axis=1
        ).astype(BF16)
        pos_chip = pos_chip + jnp.dot(place_back, both, preferred_element_type=F32)
    most = jnp.max(total, axis=1, keepdims=True)
    mark = jnp.where(most > CHIP_ROOM, float(MARK), 0.0)
    query = (low_high[:, :LANES] + low_high[:, LANES:] * float(LANES) + mark).astype(jnp.int32)
    for o in range(shards // CORES):
        queries[o] = query[o : o + 1, :]

    pl.semaphore_wait(barrier, shards - 1)
    twin = shifted(me, RING * RING, gy_size)
    lend = send(table, twin_packed, table_send, table_recv, twin, gy_size)
    lend.start()

    def ask_one(i, carry):
        peer = lax.rem(me + i, shards)
        chip, _ = chip_of(peer, gy_size)
        send(queries.at[chip], asked.at[me], ask_send, ask_recv, peer, gy_size).start()
        return carry

    lax.fori_loop(1, shards, ask_one, 0)
    own_ask = pltpu.make_async_copy(queries.at[chip_me], asked.at[me], own_sem.at[1])
    own_ask.start()

    piece = min(512, part)
    gram = jnp.zeros((LANES, LANES), F32)
    mine_from = core_me * rows_dev
    for c in range(parts):
        load(c).wait()

        def step(j, gram):
            at = c * part + j * piece
            block = packed[pl.ds(pl.multiple_of(at, piece), piece), :]
            wide[pl.ds(pl.multiple_of(mine_from + at, piece), piece), :] = block.astype(F32)
            return gram + lax.dot_general(
                block, block, (((0,), (0,)), ((), ())), preferred_element_type=F32
            )

        gram = lax.fori_loop(0, part // piece, step, gram)
    for o in range(LANES):
        terms[o] = gram[o : o + 1, :]
    exchange_rows(terms, arrived, me, shards, gy_size, term_send, term_recv)
    own_term = pltpu.make_async_copy(terms.at[me], arrived.at[me], own_sem.at[2])
    own_term.start()

    own_ask.wait()
    await_rows(asked, asked, shards, gy_size, ask_send, ask_recv)
    to_scalars = pltpu.make_async_copy(asked, asked_here, own_sem.at[3])
    to_scalars.start()
    lend.wait()
    theirs_from = (CORES - 1 - core_me) * rows_dev

    def widen(j, carry):
        at = j * piece
        block = twin_packed[pl.ds(pl.multiple_of(at, piece), piece), :]
        wide[pl.ds(pl.multiple_of(theirs_from + at, piece), piece), :] = block.astype(F32)
        return carry

    lax.fori_loop(0, rows_dev // piece, widen, 0)
    to_scalars.wait()

    my_part = core_me * ROOM
    my_place = chip_me * CORES + core_me

    def collect(peer):
        for t in range(ROOM):
            row = asked_here[peer, 0, my_part + t] & (CORES * rows_dev - 1)
            stage[pl.ds(t, 1), :] = wide[pl.ds(row, 1), :]
        outgoing[peer] = stage[...].astype(BF16)

    def serve(i, carry):
        peer = shifted(me, lax.rem(i * 37, shards), gy_size)
        collect(peer)
        send(outgoing.at[peer], landed.at[my_place], send_sem, recv_sem, peer, gy_size).start()
        return carry

    lax.fori_loop(1, shards // 2, serve, 0)
    own_term.wait()
    await_rows(terms, arrived, shards, gy_size, term_send, term_recv)
    row_total[...] = jnp.sum(arrived[...], axis=0)

    def share(i, carry):
        peer = lax.rem(me + i, shards)
        send(row_total, gramian.at[me], sum_send, sum_recv, peer, gy_size).start()
        return carry

    lax.fori_loop(1, shards, share, 0)
    own_sum = pltpu.make_async_copy(row_total, gramian.at[me], own_sem.at[4])
    own_sum.start()
    lax.fori_loop(shards // 2, shards, serve, 0)
    collect(me)
    own = pltpu.make_async_copy(outgoing.at[me], landed.at[my_place], own_sem.at[5])
    own.start()

    spot = pos_chip[:, :LANES] + pos_chip[:, LANES:] * float(CHIP_ROOM)
    spots_now = jnp.zeros((users, USER_ITEMS), F32)
    for item in range(USER_ITEMS):
        chosen = jnp.where(lane == row_index[:, item : item + 1], spot, 0.0)
        chosen = jnp.sum(chosen, axis=1, keepdims=True)
        spots_now = jnp.where(slot_lane == item, chosen, spots_now)
    spots[...] = spots_now.astype(jnp.int32)
    top[...] = jnp.max(jnp.max(asked[...], axis=0), axis=1, keepdims=True)

    own_sum.wait()
    own.wait()
    await_rows(terms, gramian, shards, gy_size, sum_send, sum_recv)
    await_rows(outgoing, landed, shards, gy_size, send_sem, recv_sem)


def solve_kernel(
    unobserved, spots, landed, gramian, confidence, counts, out, packed, wide, rows, vectors, weights, sem
):
    users = confidence.shape[0]
    parts = 8
    part = landed.shape[0] // parts

    def load(c):
        here = pl.ds(c * part, part)
        return pltpu.make_async_copy(landed.at[here], packed.at[here], sem.at[c])

    for c in range(parts):
        load(c).start()
    for c in range(parts):
        load(c).wait()
        here = pl.ds(c * part, part)
        wide[here, :] = packed[here, :].astype(F32)

    def pick(user, carry):
        for item in range(USER_ITEMS):
            rows[pl.ds(item * users + user, 1), :] = wide[pl.ds(spots[user, item], 1), :]
        return carry

    lax.fori_loop(0, users, pick, 0)
    unit = jnp.where(
        lax.broadcasted_iota(jnp.int32, (LANES, LANES), 0)
        == lax.broadcasted_iota(jnp.int32, (LANES, LANES), 1),
        1.0,
        0.0,
    ).astype(BF16)
    for item in range(USER_ITEMS):
        block = rows[pl.ds(item * users, users), :].astype(BF16)
        vectors[item] = lax.dot_general(
            unit, block, (((1,), (1,)), ((), ())), preferred_element_type=F32
        )

    item_sub = lax.broadcasted_iota(jnp.int32, (USER_ITEMS, users), 0)
    weights[...] = jnp.where(item_sub < counts[...], confidence[...].T, 0.0)
    scaled = gramian[...] * unobserved
    top = scaled.astype(BF16)
    rest = (scaled - top.astype(F32)).astype(BF16)

    right = jnp.zeros((LANES, users), F32)
    for item in range(USER_ITEMS):
        right = right + vectors[item] * weights[item : item + 1, :]
    norm = jnp.sum(right * right, axis=0, keepdims=True)

    def sweep(_, carry):
        solution, residual, direction, norm = carry
        d_top = direction.astype(BF16)
        d_rest = (direction - d_top.astype(F32)).astype(BF16)
        image = direction + (
            jnp.dot(top, d_top, preferred_element_type=F32)
            + jnp.dot(top, d_rest, preferred_element_type=F32)
            + jnp.dot(rest, d_top, preferred_element_type=F32)
        )
        for item in range(USER_ITEMS):
            vector = vectors[item]
            projected = jnp.sum(vector * direction, axis=0, keepdims=True)
            image = image + vector * (weights[item : item + 1, :] * projected)
        alpha = norm / jnp.sum(direction * image, axis=0, keepdims=True)
        solution = solution + alpha * direction
        residual = residual - alpha * image
        after = jnp.sum(residual * residual, axis=0, keepdims=True)
        direction = residual + (after / norm) * direction
        return solution, residual, direction, after

    solution, *_ = lax.fori_loop(
        0, ITERATIONS, sweep, (jnp.zeros_like(right), right, right, norm)
    )
    out[...] = solution.T


def vmem():
    return pl.BlockSpec(memory_space=pltpu.VMEM)


def smem():
    return pl.BlockSpec(memory_space=pltpu.SMEM)


def anywhere():
    return pl.BlockSpec(memory_space=pl.ANY)


def ask(shards, gy_size, blocks_dev, ids, owner_map, need):
    requests = need.shape[0]
    dma = pltpu.SemaphoreType.DMA
    return pl.pallas_call(
        functools.partial(ask_kernel, shards, gy_size, blocks_dev),
        out_shape=(
            jax.ShapeDtypeStruct((shards, 1, LANES), jnp.int32),
            jax.ShapeDtypeStruct((requests, BLOCK), jnp.int32),
            jax.ShapeDtypeStruct((1, 1), jnp.int32),
        ),
        in_specs=[smem(), anywhere(), vmem()],
        out_specs=(vmem(), vmem(), vmem()),
        scratch_shapes=[
            pltpu.VMEM(owner_map.shape, jnp.int32),
            pltpu.VMEM((requests, LANES), jnp.int32),
            pltpu.VMEM((shards, 1, LANES), jnp.int32),
            dma, dma, dma, dma,
        ],
        compiler_params=pltpu.CompilerParams(
            collective_id=1, has_side_effects=True, vmem_limit_bytes=VMEM_LIMIT
        ),
        name="ask",
    )(ids, owner_map, need)


def fetch(shards, gy_size, room, asked, table):
    dma = pltpu.SemaphoreType.DMA
    return pl.pallas_call(
        functools.partial(fetch_kernel, shards, gy_size, room),
        out_shape=(
            jax.ShapeDtypeStruct((shards, room, LANES), BF16),
            jax.ShapeDtypeStruct((shards, 1, LANES), F32),
        ),
        in_specs=[smem(), anywhere()],
        out_specs=(anywhere(), vmem()),
        scratch_shapes=[
            pltpu.VMEM(table.shape, BF16),
            pltpu.VMEM(table.shape, F32),
            pltpu.VMEM((room, LANES), F32),
            pltpu.VMEM((shards, room, LANES), BF16),
            pltpu.VMEM((shards, 1, LANES), F32),
            pltpu.VMEM((shards, 1, LANES), F32),
            pltpu.VMEM((1, LANES), F32),
            pltpu.SemaphoreType.DMA((8,)),
            pltpu.SemaphoreType.DMA((3,)),
            dma, dma, dma, dma, dma, dma,
        ],
        compiler_params=pltpu.CompilerParams(
            collective_id=2,
            has_side_effects=True,
            vmem_limit_bytes=VMEM_LIMIT,
        ),
        name="fetch",
    )(asked, table)


def gather(shards, gy_size, blocks_dev, block_ids, owner_map, slots, offsets, counts, table):
    dma = pltpu.SemaphoreType.DMA
    users = slots.shape[0]
    line = (shards, 1, LANES)
    return pl.pallas_call(
        functools.partial(gather_kernel, shards, gy_size, blocks_dev),
        out_shape=(
            jax.ShapeDtypeStruct((shards, ROOM, LANES), BF16),
            jax.ShapeDtypeStruct(line, F32),
            jax.ShapeDtypeStruct((users, USER_ITEMS), jnp.int32),
            jax.ShapeDtypeStruct((1, 1), jnp.int32),
        ),
        in_specs=[smem(), vmem(), anywhere(), vmem(), vmem(), vmem(), anywhere()],
        out_specs=(anywhere(), vmem(), vmem(), vmem()),
        scratch_shapes=[
            pltpu.VMEM(owner_map.shape, jnp.int32),
            pltpu.VMEM((users * USER_BLOCKS, LANES), jnp.int32),
            pltpu.VMEM((shards // CORES, 1, LANES), jnp.int32),
            pltpu.VMEM(line, jnp.int32),
            pltpu.SMEM(line, jnp.int32),
            pltpu.VMEM(table.shape, BF16),
            pltpu.VMEM(table.shape, BF16),
            pltpu.VMEM((CORES * table.shape[0], LANES), F32),
            pltpu.VMEM((ROOM, LANES), F32),
            pltpu.VMEM((shards, ROOM, LANES), BF16),
            pltpu.VMEM(line, F32),
            pltpu.VMEM(line, F32),
            pltpu.VMEM((1, LANES), F32),
            pltpu.SemaphoreType.DMA((8,)),
            pltpu.SemaphoreType.DMA((6,)),
            dma, dma, dma, dma, dma, dma, dma, dma, dma, dma,
        ],
        compiler_params=pltpu.CompilerParams(
            collective_id=0, has_side_effects=True, vmem_limit_bytes=VMEM_LIMIT
        ),
        name="gather",
    )(block_ids, block_ids, owner_map, slots, offsets, counts, table)


def solve(unobserved, spots, landed, gramian, confidence, counts):
    users = confidence.shape[0]
    return pl.pallas_call(
        functools.partial(solve_kernel, unobserved),
        out_shape=jax.ShapeDtypeStruct((users, LANES), F32),
        in_specs=[smem(), anywhere(), vmem(), vmem(), vmem()],
        out_specs=vmem(),
        scratch_shapes=[
            pltpu.VMEM(landed.shape, BF16),
            pltpu.VMEM(landed.shape, F32),
            pltpu.VMEM((USER_ITEMS * users, LANES), F32),
            pltpu.VMEM((USER_ITEMS, LANES, users), F32),
            pltpu.VMEM((USER_ITEMS, users), F32),
            pltpu.SemaphoreType.DMA((8,)),
        ],
        compiler_params=pltpu.CompilerParams(vmem_limit_bytes=VMEM_LIMIT),
        name="solve",
    )(spots, landed, gramian, confidence, counts)


def fetch_all(shards, gy_size, blocks_dev, item_table, block_ids, item_slots, item_offsets, item_counts, owner_map):
    users = block_ids.shape[0]
    live = jnp.arange(USER_ITEMS)[None, :] < item_counts[:, None]
    row_index = item_slots * BLOCK + item_offsets
    candidates = jnp.arange(USER_BLOCKS * BLOCK, dtype=jnp.int32)
    hits = row_index[:, :, None] == candidates[None, None, :]
    need = jnp.any(hits & live[:, :, None], axis=1).astype(F32)
    asked, keys, _ = ask(
        shards,
        gy_size,
        blocks_dev,
        block_ids.reshape(-1, LANES),
        owner_map,
        need.reshape(users * USER_BLOCKS, BLOCK),
    )
    keys = keys.reshape(users, 1, USER_BLOCKS * BLOCK)
    spots = jnp.sum(jnp.where(hits, keys, 0), axis=2)
    landed, gramian = fetch(shards, gy_size, MOST, asked.reshape(shards, LANES), item_table)
    return spots, landed, gramian


def per_device(item_table, block_ids, item_slots, item_offsets, confidence, item_counts, owner_map):
    shards, gy_size = lax.axis_size(("gx", "gy")), lax.axis_size("gy")
    rows_dev = item_table.shape[0]
    blocks_dev = rows_dev // BLOCK
    users = block_ids.shape[0]
    unobserved = USER_ITEMS / (rows_dev * shards)
    owner_map = owner_map.reshape(-1, LANES)
    counts = item_counts.reshape(1, users)

    def finish(spots, landed, gramian):
        landed = landed.reshape(-1, LANES)
        gramian = gramian.reshape(LANES, LANES)
        return solve(unobserved, spots, landed, gramian, confidence, counts)

    landed, gramian, spots, top = gather(
        shards, gy_size, blocks_dev, block_ids, owner_map,
        item_slots, item_offsets, counts, item_table,
    )
    return lax.cond(
        top[0, 0] >= MARK,
        lambda: finish(
            *fetch_all(
                shards, gy_size, blocks_dev, item_table, block_ids,
                item_slots, item_offsets, item_counts, owner_map,
            )
        ),
        lambda: finish(spots, landed, gramian),
    )


def solution(mesh):
    return jax.shard_map(
        per_device,
        mesh=mesh,
        in_specs=(
            P(("gx", "gy"), None),
            P(("gx", "gy"), None),
            P(("gx", "gy"), None),
            P(("gx", "gy"), None),
            P(("gx", "gy"), None),
            P(("gx", "gy")),
            P(),
        ),
        out_specs=P(("gx", "gy"), None),
        check_vma=False,
    )
```

```python
import functools

import jax
import jax.numpy as jnp
from jax import lax
from jax.experimental import pallas as pl
from jax.experimental.pallas import tpu as pltpu
from jax.sharding import PartitionSpec as P

BLOCK = 8
USER_BLOCKS = 8
USER_ITEMS = 32
ITERATIONS = 16
LANES = 128
CORES = 2
RING = 4
ROOM = 48
CHIP_ROOM = CORES * ROOM
MOST = 128
MARK = 1 << 20

SECOND = 64

MESH = pl.DeviceIdType.MESH
F32 = jnp.float32
BF16 = jnp.bfloat16
VMEM_LIMIT = 56 * 1024 * 1024


def place(gy_size):
    gx, gy = lax.axis_index("gx"), lax.axis_index("gy")
    return gx * gy_size + gy


def signal_all(me, shards, gy_size):
    barrier = pltpu.get_barrier_semaphore()

    def one(i, carry):
        peer = lax.rem(me + i, shards)
        pl.semaphore_signal(
            barrier,
            inc=1,
            device_id=(peer // gy_size, lax.rem(peer, gy_size)),
            device_id_type=MESH,
        )
        return carry

    lax.fori_loop(1, shards, one, 0)
    return barrier


def send(src, dst, send_sem, recv_sem, peer, gy_size):
    return pltpu.make_async_remote_copy(
        src_ref=src,
        dst_ref=dst,
        send_sem=send_sem,
        recv_sem=recv_sem,
        device_id=peer if isinstance(peer, tuple) else (peer // gy_size, lax.rem(peer, gy_size)),
        device_id_type=MESH,
    )


def exchange_rows(table, landing, me, shards, gy_size, send_sem, recv_sem):
    def one(i, carry):
        peer = lax.rem(me + i, shards)
        send(table.at[peer], landing.at[me], send_sem, recv_sem, peer, gy_size).start()
        return carry

    lax.fori_loop(1, shards, one, 0)


def await_rows(table, landing, shards, gy_size, send_sem, recv_sem):
    others = pl.ds(0, shards - 1)
    send(table.at[others], landing.at[others], send_sem, recv_sem, 0, gy_size).wait()


def ask_kernel(
    shards, gy_size, blocks_dev, ids, owner_map, need, asked, keys, top,
    owners, found, queries, map_sem, own_sem, send_sem, recv_sem,
):
    me = place(gy_size)
    barrier = signal_all(me, shards, gy_size)
    load = pltpu.make_async_copy(owner_map, owners, map_sem)
    load.start()
    requests = found.shape[0]
    lane_row = lax.broadcasted_iota(jnp.int32, (1, LANES), 1)
    load.wait()

    def look(j, carry):
        for t in range(8):
            i = j * 8 + t
            block = ids[i // LANES, lax.rem(i, LANES)]
            row = owners[pl.ds(lax.shift_right_logical(block, 7), 1), :]
            found[pl.ds(i, 1), :] = jnp.where(lane_row == (block & (LANES - 1)), row, 0)
        return carry

    lax.fori_loop(0, requests // 8, look, 0)

    chunk = LANES
    lane = lax.broadcasted_iota(jnp.int32, (chunk, LANES), 1)
    sub = lax.broadcasted_iota(jnp.int32, (chunk, LANES), 0)
    lane8 = lax.broadcasted_iota(jnp.int32, (chunk, BLOCK), 1)
    earlier = jnp.where(lane < sub, 1.0, 0.0).astype(BF16)
    total = jnp.zeros((1, LANES), F32)
    low = jnp.zeros((LANES, LANES), F32)
    high = jnp.zeros((LANES, LANES), F32)
    over_rows = (((0,), (0,)), ((), ()))
    for a in range(requests // chunk):
        rows = pl.ds(a * chunk, chunk)
        storage = jnp.sum(found[rows, :].astype(F32), axis=1, keepdims=True).astype(jnp.int32)
        owner = storage // blocks_dev
        within = storage - owner * blocks_dev
        wanted = need[rows, :]
        count = jnp.sum(wanted, axis=1, keepdims=True)
        mine = owner == lane
        one_hot = jnp.where(mine, 1.0, 0.0).astype(BF16)
        counted = jnp.where(mine, count, 0.0)
        before = jnp.dot(earlier, counted.astype(BF16), preferred_element_type=F32) + total
        start = jnp.sum(jnp.where(mine, before, 0.0), axis=1, keepdims=True).astype(jnp.int32)
        total = total + jnp.sum(counted, axis=0, keepdims=True)
        first = within * BLOCK
        low_here = jnp.zeros((chunk, LANES), F32)
        high_here = jnp.zeros((chunk, LANES), F32)
        key = jnp.zeros((chunk, BLOCK), jnp.int32)
        for r in range(BLOCK):
            live = wanted[:, r : r + 1]
            row = first + r
            hit = jnp.where(lane == start, live, 0.0)
            low_here = low_here + hit * (row & (LANES - 1)).astype(F32)
            high_here = high_here + hit * lax.shift_right_logical(row, 7).astype(F32)
            spot = jnp.where(live > 0.0, owner * MOST + start, 0)
            key = jnp.where(lane8 == r, spot, key)
            start = start + live.astype(jnp.int32)
        keys[rows, :] = key
        low = low + lax.dot_general(
            one_hot, low_here.astype(BF16), over_rows, preferred_element_type=F32
        )
        high = high + lax.dot_general(
            one_hot, high_here.astype(BF16), over_rows, preferred_element_type=F32
        )
    most = jnp.max(total, axis=1, keepdims=True)
    mark = jnp.where(most > MOST, float(MARK), 0.0)
    query = (low + high * float(LANES) + mark).astype(jnp.int32)
    for o in range(shards):
        queries[o] = query[o : o + 1, :]

    pl.semaphore_wait(barrier, shards - 1)
    exchange_rows(queries, asked, me, shards, gy_size, send_sem, recv_sem)
    own = pltpu.make_async_copy(queries.at[me], asked.at[me], own_sem)
    own.start()
    own.wait()
    await_rows(queries, asked, shards, gy_size, send_sem, recv_sem)
    top[...] = jnp.max(jnp.max(asked[...], axis=0), axis=1, keepdims=True)


def fetch_kernel(
    shards, gy_size, room, asked, table, landed, gramian,
    packed, wide, stage, outgoing, terms, arrived, row_total, table_sem, own_sem,
    send_sem, recv_sem, term_send, term_recv, sum_send, sum_recv,
):
    me = place(gy_size)
    barrier = signal_all(me, shards, gy_size)
    rows_dev = table.shape[0]
    parts = 8
    part = rows_dev // parts

    def load(c):
        rows = pl.ds(c * part, part)
        return pltpu.make_async_copy(table.at[rows], packed.at[rows], table_sem.at[c])

    for c in range(parts):
        load(c).start()
    piece = min(512, part)
    total = jnp.zeros((LANES, LANES), F32)
    for c in range(parts):
        load(c).wait()

        def step(j, total):
            rows = pl.ds(pl.multiple_of(c * part + j * piece, piece), piece)
            block = packed[rows, :]
            wide[rows, :] = block.astype(F32)
            return total + lax.dot_general(
                block, block, (((0,), (0,)), ((), ())), preferred_element_type=F32
            )

        total = lax.fori_loop(0, part // piece, step, total)
    for o in range(shards):
        terms[o] = total[o : o + 1, :]

    pl.semaphore_wait(barrier, shards - 1)
    exchange_rows(terms, arrived, me, shards, gy_size, term_send, term_recv)
    own_term = pltpu.make_async_copy(terms.at[me], arrived.at[me], own_sem.at[0])
    own_term.start()

    def collect(peer):
        for h in range(room // 16):
            for t in range(16):
                row = asked[peer, h * 16 + t] & (rows_dev - 1)
                stage[pl.ds(h * 16 + t, 1), :] = wide[pl.ds(row, 1), :]
        outgoing[peer] = stage[...].astype(BF16)

    def serve(i, carry):
        off = lax.rem(i * 37, shards)
        peer = lax.rem(me + off, shards)
        collect(peer)
        send(outgoing.at[peer], landed.at[me], send_sem, recv_sem, peer, gy_size).start()
        return carry

    lax.fori_loop(1, shards // 2, serve, 0)
    own_term.wait()
    await_rows(terms, arrived, shards, gy_size, term_send, term_recv)
    row_total[...] = jnp.sum(arrived[...], axis=0)

    def share(i, carry):
        peer = lax.rem(me + i, shards)
        send(row_total, gramian.at[me], sum_send, sum_recv, peer, gy_size).start()
        return carry

    lax.fori_loop(1, shards, share, 0)
    own_sum = pltpu.make_async_copy(row_total, gramian.at[me], own_sem.at[1])
    own_sum.start()
    lax.fori_loop(shards // 2, shards, serve, 0)
    collect(me)
    own = pltpu.make_async_copy(outgoing.at[me], landed.at[me], own_sem.at[2])
    own.start()
    own_sum.wait()
    own.wait()
    await_rows(terms, gramian, shards, gy_size, sum_send, sum_recv)
    await_rows(outgoing, landed, shards, gy_size, send_sem, recv_sem)


def bits(count):
    assert count & (count - 1) == 0
    return count.bit_length() - 1


def chip_of(device, gy_size):
    gx, gy = device // gy_size, lax.rem(device, gy_size)
    return (gx // CORES) * gy_size + gy, lax.rem(gx, CORES)


def shift_from(me, gy_size):
    gx, gy = me // gy_size, lax.rem(me, gy_size)
    y, core, x, z = gx // CORES, lax.rem(gx, CORES), gy // RING, lax.rem(gy, RING)

    def shifted(off):
        gx = lax.rem(y + off // (RING * RING * CORES), RING) * CORES
        gx = gx + lax.rem(core + off // (RING * RING), CORES)
        return gx, lax.rem(x + off // RING, RING) * RING + lax.rem(z + off, RING)

    return shifted


def gather_kernel(
    shards, gy_size, blocks_dev, ids, id_rows, owner_map, slots, offsets, counts, table,
    landed, gramian, spots, top,
    owners, found, queries, asked, asked_here, packed, twin_packed, wide, stage, outgoing,
    terms, arrived, row_total, spreads, starts, chips, load_sem, own_sem, table_send, table_recv,
    send_sem, recv_sem, ask_send, ask_recv, term_send, term_recv, sum_send, sum_recv,
):
    me = place(gy_size)
    chip_me, core_me = chip_of(me, gy_size)
    barrier = signal_all(me, shards, gy_size)
    load_map = pltpu.make_async_copy(owner_map, owners, own_sem.at[0])
    load_map.start()
    rows_dev = table.shape[0]
    parts = 8
    part = rows_dev // parts

    def load(c):
        rows = pl.ds(c * part, part)
        return pltpu.make_async_copy(table.at[rows], packed.at[rows], load_sem.at[c])

    for c in range(parts):
        load(c).start()

    users = slots.shape[1]
    requests = found.shape[0]
    group = LANES // USER_BLOCKS
    lane = lax.broadcasted_iota(jnp.int32, (LANES, LANES), 1)
    sub = lax.broadcasted_iota(jnp.int32, (LANES, LANES), 0)
    lane_f = lane.astype(F32)
    diagonal = lane == sub

    item_sub = lax.broadcasted_iota(jnp.int32, (USER_ITEMS, users), 0)
    slot_lane = lax.broadcasted_iota(jnp.int32, (users, USER_ITEMS), 1)
    row_index = slots[...] * BLOCK + offsets[...]
    row_index = jnp.where(item_sub < counts[...], row_index, -1).astype(F32)
    inner = (id_rows[...] & (LANES - 1)).astype(F32)
    by_user = jnp.concatenate(
        [row_index, inner, jnp.zeros((LANES - USER_ITEMS - USER_BLOCKS, users), F32)], axis=0
    ).T
    row_index = by_user[:, :USER_ITEMS].astype(jnp.int32)
    inner = by_user.astype(BF16)
    wanted = lane == row_index[:, 0:1]
    for item in range(1, USER_ITEMS):
        wanted = wanted | (lane == row_index[:, item : item + 1])
    wanted = jnp.where(wanted, 1.0, 0.0).astype(BF16)
    wanted_inner = jnp.concatenate([wanted, inner], axis=1)

    load_map.wait()

    def look(user, carry):
        for slot in range(USER_BLOCKS):
            line = lax.shift_right_logical(ids[slot, user], bits(LANES))
            found[pl.ds(user * USER_BLOCKS + slot, 1), :] = owners[pl.ds(line, 1), :]
        return carry

    lax.fori_loop(0, users, look, 0, unroll=2)

    same = lax.shift_right_logical(lane, 3) == (sub & 7)
    own_lane = lane == (sub & 7) + USER_ITEMS
    earlier = jnp.where(lane < sub, 1.0, 0.0).astype(BF16)
    before_row = jnp.where(
        (lax.shift_right_logical(lane, 3) == lax.shift_right_logical(sub, 3))
        & ((sub & 7) < (lane & 7)),
        1.0,
        0.0,
    ).astype(BF16)
    up_to = jnp.concatenate(
        [jnp.where((sub & 7) <= r, 1.0, 0.0).astype(BF16) for r in range(BLOCK)], axis=1
    )
    total = jnp.zeros((1, LANES), F32)
    low_high = jnp.zeros((LANES, 2 * LANES), F32)
    for a in range(requests // LANES):
        pick = jnp.where(lax.shift_right_logical(sub, bits(USER_BLOCKS)) + a * group == lane, 1.0, 0.0).astype(BF16)
        picked = jnp.dot(pick, wanted_inner, preferred_element_type=F32)
        spread = jnp.where(same, picked[:, :LANES], 0.0).astype(BF16)
        inner_here = jnp.sum(jnp.where(own_lane, picked[:, LANES:], 0.0), axis=1, keepdims=True)
        line = found[pl.ds(a * LANES, LANES), :].astype(F32)
        storage = jnp.sum(jnp.where(lane_f == inner_here, line, 0.0), axis=1, keepdims=True)
        storage = storage.astype(jnp.int32)
        device = lax.shift_right_logical(storage, bits(blocks_dev))
        within = storage & (blocks_dev - 1)
        gx = lax.shift_right_logical(device, bits(gy_size))
        chip = lax.shift_right_logical(gx, bits(CORES)) * gy_size + (device & (gy_size - 1))
        core = gx & (CORES - 1)
        low_first = ((within & 15) * BLOCK).astype(F32)
        high = (core * (rows_dev // LANES) + lax.shift_right_logical(within, 4)).astype(F32)
        chip = chip.astype(F32)
        so_far = jnp.dot(spread, up_to, preferred_element_type=F32)
        so_far = [so_far[:, r * LANES : (r + 1) * LANES] for r in range(BLOCK)]
        mine = lane_f == chip
        counted = jnp.where(mine, so_far[-1], 0.0)
        before = jnp.dot(earlier, counted.astype(BF16), preferred_element_type=F32) + total
        start = jnp.sum(jnp.where(mine, before, 0.0), axis=1, keepdims=True)
        total = total + jnp.sum(counted, axis=0, keepdims=True)
        depth = lane_f - start
        which = jnp.zeros((LANES, LANES), F32)
        for m in so_far:
            which = which + jnp.where(m <= depth, 1.0, 0.0)
        hit = (depth >= 0.0) & (depth < so_far[-1])
        both = jnp.concatenate(
            [jnp.where(hit, low_first + which, 0.0), jnp.where(hit, high, 0.0)], axis=1
        ).astype(BF16)
        chip_row = jnp.sum(jnp.where(diagonal, chip, 0.0), axis=0, keepdims=True)
        to_chip = jnp.where(sub.astype(F32) == chip_row, 1.0, 0.0).astype(BF16)
        low_high = low_high + jnp.dot(to_chip, both, preferred_element_type=F32)
        here = pl.ds(a * LANES, LANES)
        spreads[here, :] = spread
        starts[here, :] = jnp.broadcast_to(start, (LANES, LANES))
        chips[here, :] = jnp.broadcast_to(chip, (LANES, LANES))
    most = jnp.max(total, axis=1, keepdims=True)
    mark = jnp.where(most > CHIP_ROOM, float(MARK), 0.0)
    query = (low_high[:, :LANES] + low_high[:, LANES:] * float(LANES) + mark).astype(jnp.int32)
    for core in range(CORES):
        shares = pltpu.roll(query, LANES - core * ROOM, 1) if core else query
        for o in range(shards // CORES):
            device = (o // gy_size * CORES + core) * gy_size + o % gy_size
            queries[device] = shares[o : o + 1, :]

    piece = min(512, rows_dev)
    mine_from = core_me * rows_dev
    theirs_from = (CORES - 1 - core_me) * rows_dev

    def widen(source, start, j, carry):
        at = j * piece
        block = source[pl.ds(pl.multiple_of(at, piece), piece), :]
        wide[pl.ds(pl.multiple_of(start + at, piece), piece), :] = block.astype(F32)
        return carry

    for c in range(parts):
        load(c).wait()
    lax.fori_loop(0, rows_dev // piece, functools.partial(widen, packed, mine_from), 0)

    pl.semaphore_wait(barrier, shards - 1)
    shifted = shift_from(me, gy_size)
    twin = shifted(RING * RING)
    lend = send(table, twin_packed, table_send, table_recv, twin, gy_size)
    exchange_rows(queries, asked, me, shards, gy_size, ask_send, ask_recv)
    lend.start()
    own_ask = pltpu.make_async_copy(queries.at[me], asked.at[me], own_sem.at[1])
    own_ask.start()

    def step(j, gram):
        block = packed[pl.ds(pl.multiple_of(j * piece, piece), piece), :]
        return gram + lax.dot_general(
            block, block, (((0,), (0,)), ((), ())), preferred_element_type=F32
        )

    gram = lax.fori_loop(0, rows_dev // piece, step, jnp.zeros((LANES, LANES), F32))
    for o in range(LANES):
        terms[o] = gram[o : o + 1, :]
    exchange_rows(terms, arrived, me, shards, gy_size, term_send, term_recv)
    own_term = pltpu.make_async_copy(terms.at[me], arrived.at[me], own_sem.at[2])
    own_term.start()

    own_ask.wait()
    await_rows(asked, asked, shards, gy_size, ask_send, ask_recv)
    to_scalars = pltpu.make_async_copy(asked, asked_here, own_sem.at[3])
    to_scalars.start()
    lend.wait()
    lax.fori_loop(0, rows_dev // piece, functools.partial(widen, twin_packed, theirs_from), 0)
    to_scalars.wait()

    my_place = chip_me * CORES + core_me

    def collect(peer):
        for t in range(ROOM):
            row = asked_here[peer, 0, t] & (CORES * rows_dev - 1)
            stage[pl.ds(t, 1), :] = wide[pl.ds(row, 1), :]
        outgoing[peer] = stage[...].astype(BF16)

    def serve(i, carry):
        gx, gy = shifted(lax.rem(i * 37, shards))
        peer = gx * gy_size + gy
        collect(peer)
        send(outgoing.at[peer], landed.at[my_place], send_sem, recv_sem, (gx, gy), gy_size).start()
        return carry

    lax.fori_loop(1, SECOND, serve, 0)
    own_term.wait()
    await_rows(terms, arrived, shards, gy_size, term_send, term_recv)
    row_total[...] = jnp.sum(arrived[...], axis=0)

    def share(i, carry):
        peer = lax.rem(me + i, shards)
        send(row_total, gramian.at[me], sum_send, sum_recv, peer, gy_size).start()
        return carry

    lax.fori_loop(1, shards, share, 0)
    own_sum = pltpu.make_async_copy(row_total, gramian.at[me], own_sem.at[4])
    own_sum.start()
    lax.fori_loop(SECOND, shards, serve, 0)
    collect(me)
    own = pltpu.make_async_copy(outgoing.at[me], landed.at[my_place], own_sem.at[5])
    own.start()

    pos_chip = jnp.zeros((users, 2 * LANES), F32)
    for a in range(requests // LANES):
        here = pl.ds(a * LANES, LANES)
        back = lax.shift_right_logical(lane, bits(USER_BLOCKS)) + a * group == sub
        spread = spreads[here, :]
        live = spread.astype(F32) > 0.0
        spot = jnp.dot(spread, before_row, preferred_element_type=F32) + starts[here, :]
        both = jnp.concatenate(
            [jnp.where(live, spot, 0.0), jnp.where(live, chips[here, :], 0.0)], axis=1
        ).astype(BF16)
        back = jnp.where(back, 1.0, 0.0).astype(BF16)
        pos_chip = pos_chip + jnp.dot(back, both, preferred_element_type=F32)
    spot = pos_chip[:, :LANES] + pos_chip[:, LANES:] * float(CHIP_ROOM)
    spots_now = jnp.zeros((users, USER_ITEMS), F32)
    for item in range(USER_ITEMS):
        chosen = jnp.where(lane == row_index[:, item : item + 1], spot, 0.0)
        chosen = jnp.sum(chosen, axis=1, keepdims=True)
        spots_now = jnp.where(slot_lane == item, chosen, spots_now)
    spots[...] = spots_now.astype(jnp.int32)
    top[...] = jnp.max(jnp.max(asked[...], axis=0), axis=1, keepdims=True)

    own_sum.wait()
    own.wait()
    await_rows(terms, gramian, shards, gy_size, sum_send, sum_recv)
    await_rows(outgoing, landed, shards, gy_size, send_sem, recv_sem)


def solve_kernel(
    unobserved, spots, landed, gramian, confidence, counts, out, packed, wide, rows, vectors, weights, sem
):
    users = confidence.shape[1]
    parts = 8
    part = landed.shape[0] // parts

    def load(c):
        here = pl.ds(c * part, part)
        return pltpu.make_async_copy(landed.at[here], packed.at[here], sem.at[c])

    for c in range(parts):
        load(c).start()
    for c in range(parts):
        load(c).wait()
        here = pl.ds(c * part, part)
        wide[here, :] = packed[here, :].astype(F32)

    def pick(user, carry):
        for item in range(USER_ITEMS):
            rows[pl.ds(item * users + user, 1), :] = wide[pl.ds(spots[user, item], 1), :]
        return carry

    lax.fori_loop(0, users, pick, 0)
    unit = jnp.where(
        lax.broadcasted_iota(jnp.int32, (LANES, LANES), 0)
        == lax.broadcasted_iota(jnp.int32, (LANES, LANES), 1),
        1.0,
        0.0,
    ).astype(BF16)
    for item in range(USER_ITEMS):
        block = rows[pl.ds(item * users, users), :].astype(BF16)
        vectors[item] = lax.dot_general(
            unit, block, (((1,), (1,)), ((), ())), preferred_element_type=F32
        )

    item_sub = lax.broadcasted_iota(jnp.int32, (USER_ITEMS, users), 0)
    weights[...] = jnp.where(item_sub < counts[...], confidence[...], 0.0)
    scaled = gramian[...] * unobserved
    top = scaled.astype(BF16)
    rest = (scaled - top.astype(F32)).astype(BF16)

    right = jnp.zeros((LANES, users), F32)
    for item in range(USER_ITEMS):
        right = right + vectors[item] * weights[item : item + 1, :]
    norm = jnp.sum(right * right, axis=0, keepdims=True)

    def sweep(_, carry):
        solution, residual, direction, norm = carry
        d_top = direction.astype(BF16)
        d_rest = (direction - d_top.astype(F32)).astype(BF16)
        image = direction + (
            jnp.dot(top, d_top, preferred_element_type=F32)
            + jnp.dot(top, d_rest, preferred_element_type=F32)
            + jnp.dot(rest, d_top, preferred_element_type=F32)
        )
        for item in range(USER_ITEMS):
            vector = vectors[item]
            projected = jnp.sum(vector * direction, axis=0, keepdims=True)
            image = image + vector * (weights[item : item + 1, :] * projected)
        alpha = norm / jnp.sum(direction * image, axis=0, keepdims=True)
        solution = solution + alpha * direction
        residual = residual - alpha * image
        after = jnp.sum(residual * residual, axis=0, keepdims=True)
        direction = residual + (after / norm) * direction
        return solution, residual, direction, after

    solution, *_ = lax.fori_loop(
        0, ITERATIONS, sweep, (jnp.zeros_like(right), right, right, norm)
    )
    out[...] = solution.T


def vmem():
    return pl.BlockSpec(memory_space=pltpu.VMEM)


def smem():
    return pl.BlockSpec(memory_space=pltpu.SMEM)


def anywhere():
    return pl.BlockSpec(memory_space=pl.ANY)


def ask(shards, gy_size, blocks_dev, ids, owner_map, need):
    requests = need.shape[0]
    dma = pltpu.SemaphoreType.DMA
    return pl.pallas_call(
        functools.partial(ask_kernel, shards, gy_size, blocks_dev),
        out_shape=(
            jax.ShapeDtypeStruct((shards, 1, LANES), jnp.int32),
            jax.ShapeDtypeStruct((requests, BLOCK), jnp.int32),
            jax.ShapeDtypeStruct((1, 1), jnp.int32),
        ),
        in_specs=[smem(), anywhere(), vmem()],
        out_specs=(vmem(), vmem(), vmem()),
        scratch_shapes=[
            pltpu.VMEM(owner_map.shape, jnp.int32),
            pltpu.VMEM((requests, LANES), jnp.int32),
            pltpu.VMEM((shards, 1, LANES), jnp.int32),
            dma, dma, dma, dma,
        ],
        compiler_params=pltpu.CompilerParams(
            collective_id=1, has_side_effects=True, vmem_limit_bytes=VMEM_LIMIT
        ),
        name="ask",
    )(ids, owner_map, need)


def fetch(shards, gy_size, room, asked, table):
    dma = pltpu.SemaphoreType.DMA
    return pl.pallas_call(
        functools.partial(fetch_kernel, shards, gy_size, room),
        out_shape=(
            jax.ShapeDtypeStruct((shards, room, LANES), BF16),
            jax.ShapeDtypeStruct((shards, 1, LANES), F32),
        ),
        in_specs=[smem(), anywhere()],
        out_specs=(anywhere(), vmem()),
        scratch_shapes=[
            pltpu.VMEM(table.shape, BF16),
            pltpu.VMEM(table.shape, F32),
            pltpu.VMEM((room, LANES), F32),
            pltpu.VMEM((shards, room, LANES), BF16),
            pltpu.VMEM((shards, 1, LANES), F32),
            pltpu.VMEM((shards, 1, LANES), F32),
            pltpu.VMEM((1, LANES), F32),
            pltpu.SemaphoreType.DMA((8,)),
            pltpu.SemaphoreType.DMA((3,)),
            dma, dma, dma, dma, dma, dma,
        ],
        compiler_params=pltpu.CompilerParams(
            collective_id=2,
            has_side_effects=True,
            vmem_limit_bytes=VMEM_LIMIT,
        ),
        name="fetch",
    )(asked, table)


def gather(shards, gy_size, blocks_dev, block_ids, owner_map, slots, offsets, counts, table):
    dma = pltpu.SemaphoreType.DMA
    users = slots.shape[1]
    line = (shards, 1, LANES)
    return pl.pallas_call(
        functools.partial(gather_kernel, shards, gy_size, blocks_dev),
        out_shape=(
            jax.ShapeDtypeStruct((shards, ROOM, LANES), BF16),
            jax.ShapeDtypeStruct(line, F32),
            jax.ShapeDtypeStruct((users, USER_ITEMS), jnp.int32),
            jax.ShapeDtypeStruct((1, 1), jnp.int32),
        ),
        in_specs=[smem(), vmem(), anywhere(), vmem(), vmem(), vmem(), anywhere()],
        out_specs=(anywhere(), vmem(), vmem(), vmem()),
        scratch_shapes=[
            pltpu.VMEM(owner_map.shape, jnp.int32),
            pltpu.VMEM((users * USER_BLOCKS, LANES), jnp.int32),
            pltpu.VMEM(line, jnp.int32),
            pltpu.VMEM(line, jnp.int32),
            pltpu.SMEM(line, jnp.int32),
            pltpu.VMEM(table.shape, BF16),
            pltpu.VMEM(table.shape, BF16),
            pltpu.VMEM((CORES * table.shape[0], LANES), F32),
            pltpu.VMEM((ROOM, LANES), F32),
            pltpu.VMEM((shards, ROOM, LANES), BF16),
            pltpu.VMEM(line, F32),
            pltpu.VMEM(line, F32),
            pltpu.VMEM((1, LANES), F32),
            pltpu.VMEM((users * USER_BLOCKS, LANES), BF16),
            pltpu.VMEM((users * USER_BLOCKS, LANES), F32),
            pltpu.VMEM((users * USER_BLOCKS, LANES), F32),
            pltpu.SemaphoreType.DMA((8,)),
            pltpu.SemaphoreType.DMA((6,)),
            dma, dma, dma, dma, dma, dma, dma, dma, dma, dma,
        ],
        compiler_params=pltpu.CompilerParams(
            collective_id=0, has_side_effects=True, vmem_limit_bytes=VMEM_LIMIT
        ),
        name="gather",
    )(block_ids, block_ids, owner_map, slots, offsets, counts, table)


def solve(unobserved, spots, landed, gramian, confidence, counts):
    users = confidence.shape[1]
    return pl.pallas_call(
        functools.partial(solve_kernel, unobserved),
        out_shape=jax.ShapeDtypeStruct((users, LANES), F32),
        in_specs=[smem(), anywhere(), vmem(), vmem(), vmem()],
        out_specs=vmem(),
        scratch_shapes=[
            pltpu.VMEM(landed.shape, BF16),
            pltpu.VMEM(landed.shape, F32),
            pltpu.VMEM((USER_ITEMS * users, LANES), F32),
            pltpu.VMEM((USER_ITEMS, LANES, users), F32),
            pltpu.VMEM((USER_ITEMS, users), F32),
            pltpu.SemaphoreType.DMA((8,)),
        ],
        compiler_params=pltpu.CompilerParams(vmem_limit_bytes=VMEM_LIMIT),
        name="solve",
    )(spots, landed, gramian, confidence, counts)


def fetch_all(shards, gy_size, blocks_dev, item_table, block_ids, item_slots, item_offsets, item_counts, owner_map):
    users = block_ids.shape[0]
    live = jnp.arange(USER_ITEMS)[None, :] < item_counts[:, None]
    row_index = item_slots * BLOCK + item_offsets
    candidates = jnp.arange(USER_BLOCKS * BLOCK, dtype=jnp.int32)
    hits = row_index[:, :, None] == candidates[None, None, :]
    need = jnp.any(hits & live[:, :, None], axis=1).astype(F32)
    asked, keys, _ = ask(
        shards,
        gy_size,
        blocks_dev,
        block_ids.reshape(-1, LANES),
        owner_map,
        need.reshape(users * USER_BLOCKS, BLOCK),
    )
    keys = keys.reshape(users, 1, USER_BLOCKS * BLOCK)
    spots = jnp.sum(jnp.where(hits, keys, 0), axis=2)
    landed, gramian = fetch(shards, gy_size, MOST, asked.reshape(shards, LANES), item_table)
    return spots, landed, gramian


def per_device(item_table, block_ids, item_slots, item_offsets, confidence, item_counts, owner_map):
    shards, gy_size = lax.axis_size(("gx", "gy")), lax.axis_size("gy")
    rows_dev = item_table.shape[0]
    blocks_dev = rows_dev // BLOCK
    users = block_ids.shape[0]
    unobserved = USER_ITEMS / (rows_dev * shards)
    owner_map = owner_map.reshape(-1, LANES)
    counts = item_counts.reshape(1, users)

    def finish(spots, landed, gramian):
        landed = landed.reshape(-1, LANES)
        gramian = gramian.reshape(LANES, LANES)
        return solve(unobserved, spots, landed, gramian, confidence.T, counts)

    landed, gramian, spots, top = gather(
        shards, gy_size, blocks_dev, block_ids.T, owner_map,
        item_slots.T, item_offsets.T, counts, item_table,
    )
    return lax.cond(
        top[0, 0] >= MARK,
        lambda: finish(
            *fetch_all(
                shards, gy_size, blocks_dev, item_table, block_ids,
                item_slots, item_offsets, item_counts, owner_map,
            )
        ),
        lambda: finish(spots, landed, gramian),
    )


def solution(mesh):
    return jax.shard_map(
        per_device,
        mesh=mesh,
        in_specs=(
            P(("gx", "gy"), None),
            P(("gx", "gy"), None),
            P(("gx", "gy"), None),
            P(("gx", "gy"), None),
            P(("gx", "gy"), None),
            P(("gx", "gy")),
            P(),
        ),
        out_specs=P(("gx", "gy"), None),
        check_vma=False,
    )
```

```python
import functools

import jax
import jax.numpy as jnp
from jax import lax
from jax.experimental import pallas as pl
from jax.experimental.pallas import tpu as pltpu
from jax.sharding import PartitionSpec as P

BLOCK = 8
USER_BLOCKS = 8
USER_ITEMS = 32
ITERATIONS = 16
LANES = 128
CORES = 2
RING = 4
ROOM = 48
CHIP_ROOM = CORES * ROOM
MOST = 128
MARK = 1 << 20

SECOND = 64

MESH = pl.DeviceIdType.MESH
F32 = jnp.float32
BF16 = jnp.bfloat16
VMEM_LIMIT = 56 * 1024 * 1024


def place(gy_size):
    gx, gy = lax.axis_index("gx"), lax.axis_index("gy")
    return gx * gy_size + gy


def signal_all(me, shards, gy_size):
    barrier = pltpu.get_barrier_semaphore()

    def one(i, carry):
        peer = lax.rem(me + i, shards)
        pl.semaphore_signal(
            barrier,
            inc=1,
            device_id=(peer // gy_size, lax.rem(peer, gy_size)),
            device_id_type=MESH,
        )
        return carry

    lax.fori_loop(1, shards, one, 0)
    return barrier


def send(src, dst, send_sem, recv_sem, peer, gy_size):
    return pltpu.make_async_remote_copy(
        src_ref=src,
        dst_ref=dst,
        send_sem=send_sem,
        recv_sem=recv_sem,
        device_id=peer if isinstance(peer, tuple) else (peer // gy_size, lax.rem(peer, gy_size)),
        device_id_type=MESH,
    )


def exchange_rows(table, landing, me, shards, gy_size, send_sem, recv_sem):
    def one(i, carry):
        peer = lax.rem(me + i, shards)
        send(table.at[peer], landing.at[me], send_sem, recv_sem, peer, gy_size).start()
        return carry

    lax.fori_loop(1, shards, one, 0)


def await_rows(table, landing, shards, gy_size, send_sem, recv_sem):
    others = pl.ds(0, shards - 1)
    send(table.at[others], landing.at[others], send_sem, recv_sem, 0, gy_size).wait()


def ask_kernel(
    shards, gy_size, blocks_dev, ids, owner_map, need, asked, keys, top,
    owners, found, queries, map_sem, own_sem, send_sem, recv_sem,
):
    me = place(gy_size)
    barrier = signal_all(me, shards, gy_size)
    load = pltpu.make_async_copy(owner_map, owners, map_sem)
    load.start()
    requests = found.shape[0]
    lane_row = lax.broadcasted_iota(jnp.int32, (1, LANES), 1)
    load.wait()

    def look(j, carry):
        for t in range(8):
            i = j * 8 + t
            block = ids[i // LANES, lax.rem(i, LANES)]
            row = owners[pl.ds(lax.shift_right_logical(block, 7), 1), :]
            found[pl.ds(i, 1), :] = jnp.where(lane_row == (block & (LANES - 1)), row, 0)
        return carry

    lax.fori_loop(0, requests // 8, look, 0)

    chunk = LANES
    lane = lax.broadcasted_iota(jnp.int32, (chunk, LANES), 1)
    sub = lax.broadcasted_iota(jnp.int32, (chunk, LANES), 0)
    lane8 = lax.broadcasted_iota(jnp.int32, (chunk, BLOCK), 1)
    earlier = jnp.where(lane < sub, 1.0, 0.0).astype(BF16)
    total = jnp.zeros((1, LANES), F32)
    low = jnp.zeros((LANES, LANES), F32)
    high = jnp.zeros((LANES, LANES), F32)
    over_rows = (((0,), (0,)), ((), ()))
    for a in range(requests // chunk):
        rows = pl.ds(a * chunk, chunk)
        storage = jnp.sum(found[rows, :].astype(F32), axis=1, keepdims=True).astype(jnp.int32)
        owner = storage // blocks_dev
        within = storage - owner * blocks_dev
        wanted = need[rows, :]
        count = jnp.sum(wanted, axis=1, keepdims=True)
        mine = owner == lane
        one_hot = jnp.where(mine, 1.0, 0.0).astype(BF16)
        counted = jnp.where(mine, count, 0.0)
        before = jnp.dot(earlier, counted.astype(BF16), preferred_element_type=F32) + total
        start = jnp.sum(jnp.where(mine, before, 0.0), axis=1, keepdims=True).astype(jnp.int32)
        total = total + jnp.sum(counted, axis=0, keepdims=True)
        first = within * BLOCK
        low_here = jnp.zeros((chunk, LANES), F32)
        high_here = jnp.zeros((chunk, LANES), F32)
        key = jnp.zeros((chunk, BLOCK), jnp.int32)
        for r in range(BLOCK):
            live = wanted[:, r : r + 1]
            row = first + r
            hit = jnp.where(lane == start, live, 0.0)
            low_here = low_here + hit * (row & (LANES - 1)).astype(F32)
            high_here = high_here + hit * lax.shift_right_logical(row, 7).astype(F32)
            spot = jnp.where(live > 0.0, owner * MOST + start, 0)
            key = jnp.where(lane8 == r, spot, key)
            start = start + live.astype(jnp.int32)
        keys[rows, :] = key
        low = low + lax.dot_general(
            one_hot, low_here.astype(BF16), over_rows, preferred_element_type=F32
        )
        high = high + lax.dot_general(
            one_hot, high_here.astype(BF16), over_rows, preferred_element_type=F32
        )
    most = jnp.max(total, axis=1, keepdims=True)
    mark = jnp.where(most > MOST, float(MARK), 0.0)
    query = (low + high * float(LANES) + mark).astype(jnp.int32)
    for o in range(shards):
        queries[o] = query[o : o + 1, :]

    pl.semaphore_wait(barrier, shards - 1)
    exchange_rows(queries, asked, me, shards, gy_size, send_sem, recv_sem)
    own = pltpu.make_async_copy(queries.at[me], asked.at[me], own_sem)
    own.start()
    own.wait()
    await_rows(queries, asked, shards, gy_size, send_sem, recv_sem)
    top[...] = jnp.max(jnp.max(asked[...], axis=0), axis=1, keepdims=True)


def fetch_kernel(
    shards, gy_size, room, asked, table, landed, gramian,
    packed, wide, stage, outgoing, terms, arrived, row_total, table_sem, own_sem,
    send_sem, recv_sem, term_send, term_recv, sum_send, sum_recv,
):
    me = place(gy_size)
    barrier = signal_all(me, shards, gy_size)
    rows_dev = table.shape[0]
    parts = 8
    part = rows_dev // parts

    def load(c):
        rows = pl.ds(c * part, part)
        return pltpu.make_async_copy(table.at[rows], packed.at[rows], table_sem.at[c])

    for c in range(parts):
        load(c).start()
    piece = min(512, part)
    total = jnp.zeros((LANES, LANES), F32)
    for c in range(parts):
        load(c).wait()

        def step(j, total):
            rows = pl.ds(pl.multiple_of(c * part + j * piece, piece), piece)
            block = packed[rows, :]
            wide[rows, :] = block.astype(F32)
            return total + lax.dot_general(
                block, block, (((0,), (0,)), ((), ())), preferred_element_type=F32
            )

        total = lax.fori_loop(0, part // piece, step, total)
    for o in range(shards):
        terms[o] = total[o : o + 1, :]

    pl.semaphore_wait(barrier, shards - 1)
    exchange_rows(terms, arrived, me, shards, gy_size, term_send, term_recv)
    own_term = pltpu.make_async_copy(terms.at[me], arrived.at[me], own_sem.at[0])
    own_term.start()

    def collect(peer):
        for h in range(room // 16):
            for t in range(16):
                row = asked[peer, h * 16 + t] & (rows_dev - 1)
                stage[pl.ds(h * 16 + t, 1), :] = wide[pl.ds(row, 1), :]
        outgoing[peer] = stage[...].astype(BF16)

    def serve(i, carry):
        off = lax.rem(i * 77, shards)
        peer = lax.rem(me + off, shards)
        collect(peer)
        send(outgoing.at[peer], landed.at[me], send_sem, recv_sem, peer, gy_size).start()
        return carry

    lax.fori_loop(1, shards // 2, serve, 0)
    own_term.wait()
    await_rows(terms, arrived, shards, gy_size, term_send, term_recv)
    row_total[...] = jnp.sum(arrived[...], axis=0)

    def share(i, carry):
        peer = lax.rem(me + i, shards)
        send(row_total, gramian.at[me], sum_send, sum_recv, peer, gy_size).start()
        return carry

    lax.fori_loop(1, shards, share, 0)
    own_sum = pltpu.make_async_copy(row_total, gramian.at[me], own_sem.at[1])
    own_sum.start()
    lax.fori_loop(shards // 2, shards, serve, 0)
    collect(me)
    own = pltpu.make_async_copy(outgoing.at[me], landed.at[me], own_sem.at[2])
    own.start()
    own_sum.wait()
    own.wait()
    await_rows(terms, gramian, shards, gy_size, sum_send, sum_recv)
    await_rows(outgoing, landed, shards, gy_size, send_sem, recv_sem)


def bits(count):
    assert count & (count - 1) == 0
    return count.bit_length() - 1


def chip_of(device, gy_size):
    gx, gy = device // gy_size, lax.rem(device, gy_size)
    return (gx // CORES) * gy_size + gy, lax.rem(gx, CORES)


def shift_from(me, gy_size):
    gx, gy = me // gy_size, lax.rem(me, gy_size)
    y, core, x, z = gx // CORES, lax.rem(gx, CORES), gy // RING, lax.rem(gy, RING)

    def shifted(off):
        gx = lax.rem(y + off // (RING * RING * CORES), RING) * CORES
        gx = gx + lax.rem(core + off // (RING * RING), CORES)
        return gx, lax.rem(x + off // RING, RING) * RING + lax.rem(z + off, RING)

    return shifted


def conjugate(unobserved, gramian, confidence, counts, out, rows, vectors, weights):
    users = confidence.shape[1]
    unit = jnp.where(
        lax.broadcasted_iota(jnp.int32, (LANES, LANES), 0)
        == lax.broadcasted_iota(jnp.int32, (LANES, LANES), 1),
        1.0,
        0.0,
    ).astype(BF16)
    for item in range(USER_ITEMS):
        block = rows[pl.ds(item * users, users), :].astype(BF16)
        vectors[item] = lax.dot_general(
            unit, block, (((1,), (1,)), ((), ())), preferred_element_type=F32
        )

    item_sub = lax.broadcasted_iota(jnp.int32, (USER_ITEMS, users), 0)
    weights[...] = jnp.where(item_sub < counts[...], confidence[...], 0.0)
    scaled = gramian * unobserved
    top = scaled.astype(BF16)
    rest = (scaled - top.astype(F32)).astype(BF16)

    right = jnp.zeros((LANES, users), F32)
    for item in range(USER_ITEMS):
        right = right + vectors[item] * weights[item : item + 1, :]
    norm = jnp.sum(right * right, axis=0, keepdims=True)

    def sweep(_, carry):
        solution, residual, direction, norm = carry
        d_top = direction.astype(BF16)
        d_rest = (direction - d_top.astype(F32)).astype(BF16)
        image = direction + (
            jnp.dot(top, d_top, preferred_element_type=F32)
            + jnp.dot(top, d_rest, preferred_element_type=F32)
            + jnp.dot(rest, d_top, preferred_element_type=F32)
        )
        for item in range(USER_ITEMS):
            vector = vectors[item]
            projected = jnp.sum(vector * direction, axis=0, keepdims=True)
            image = image + vector * (weights[item : item + 1, :] * projected)
        alpha = norm / jnp.sum(direction * image, axis=0, keepdims=True)
        solution = solution + alpha * direction
        residual = residual - alpha * image
        after = jnp.sum(residual * residual, axis=0, keepdims=True)
        direction = residual + (after / norm) * direction
        return solution, residual, direction, after

    solution, *_ = lax.fori_loop(
        0, ITERATIONS, sweep, (jnp.zeros_like(right), right, right, norm)
    )
    out[...] = solution.T


def gather_kernel(
    shards, gy_size, blocks_dev, unobserved,
    ids, id_rows, owner_map, slots, offsets, counts, confidence, table, out, top,
    owners, found, queries, asked, asked_here, packed, twin_packed, wide, stage, outgoing,
    terms, arrived, row_total, spreads, starts, chips,
    landed, gramian, spots, spots_here, rows, vectors, weights, load_sem, own_sem, table_send, table_recv,
    send_sem, recv_sem, ask_send, ask_recv, term_send, term_recv, sum_send, sum_recv,
):
    me = place(gy_size)
    chip_me, core_me = chip_of(me, gy_size)
    barrier = signal_all(me, shards, gy_size)
    load_map = pltpu.make_async_copy(owner_map, owners, own_sem.at[0])
    load_map.start()
    rows_dev = table.shape[0]
    parts = 8
    part = rows_dev // parts

    def load(c):
        rows = pl.ds(c * part, part)
        return pltpu.make_async_copy(table.at[rows], packed.at[rows], load_sem.at[c])

    for c in range(parts):
        load(c).start()

    users = slots.shape[1]
    requests = found.shape[0]
    group = LANES // USER_BLOCKS
    lane = lax.broadcasted_iota(jnp.int32, (LANES, LANES), 1)
    sub = lax.broadcasted_iota(jnp.int32, (LANES, LANES), 0)
    lane_f = lane.astype(F32)
    diagonal = lane == sub

    item_sub = lax.broadcasted_iota(jnp.int32, (USER_ITEMS, users), 0)
    slot_lane = lax.broadcasted_iota(jnp.int32, (users, USER_ITEMS), 1)
    row_index = slots[...] * BLOCK + offsets[...]
    row_index = jnp.where(item_sub < counts[...], row_index, -1).astype(F32)
    inner = (id_rows[...] & (LANES - 1)).astype(F32)
    by_user = jnp.concatenate(
        [row_index, inner, jnp.zeros((LANES - USER_ITEMS - USER_BLOCKS, users), F32)], axis=0
    ).T
    row_index = by_user[:, :USER_ITEMS].astype(jnp.int32)
    inner = by_user.astype(BF16)
    wanted = lane == row_index[:, 0:1]
    for item in range(1, USER_ITEMS):
        wanted = wanted | (lane == row_index[:, item : item + 1])
    wanted = jnp.where(wanted, 1.0, 0.0).astype(BF16)
    wanted_inner = jnp.concatenate([wanted, inner], axis=1)

    load_map.wait()

    def look(user, carry):
        for slot in range(USER_BLOCKS):
            line = lax.shift_right_logical(ids[slot, user], bits(LANES))
            found[pl.ds(user * USER_BLOCKS + slot, 1), :] = owners[pl.ds(line, 1), :]
        return carry

    lax.fori_loop(0, users, look, 0, unroll=2)

    same = lax.shift_right_logical(lane, 3) == (sub & 7)
    own_lane = lane == (sub & 7) + USER_ITEMS
    earlier = jnp.where(lane < sub, 1.0, 0.0).astype(BF16)
    before_row = jnp.where(
        (lax.shift_right_logical(lane, 3) == lax.shift_right_logical(sub, 3))
        & ((sub & 7) < (lane & 7)),
        1.0,
        0.0,
    ).astype(BF16)
    up_to = jnp.concatenate(
        [jnp.where((sub & 7) <= r, 1.0, 0.0).astype(BF16) for r in range(BLOCK)], axis=1
    )
    total = jnp.zeros((1, LANES), F32)
    low_high = jnp.zeros((LANES, 2 * LANES), F32)
    for a in range(requests // LANES):
        pick = jnp.where(lax.shift_right_logical(sub, bits(USER_BLOCKS)) + a * group == lane, 1.0, 0.0).astype(BF16)
        picked = jnp.dot(pick, wanted_inner, preferred_element_type=F32)
        spread = jnp.where(same, picked[:, :LANES], 0.0).astype(BF16)
        inner_here = jnp.sum(jnp.where(own_lane, picked[:, LANES:], 0.0), axis=1, keepdims=True)
        line = found[pl.ds(a * LANES, LANES), :].astype(F32)
        storage = jnp.sum(jnp.where(lane_f == inner_here, line, 0.0), axis=1, keepdims=True)
        storage = storage.astype(jnp.int32)
        device = lax.shift_right_logical(storage, bits(blocks_dev))
        within = storage & (blocks_dev - 1)
        gx = lax.shift_right_logical(device, bits(gy_size))
        chip = lax.shift_right_logical(gx, bits(CORES)) * gy_size + (device & (gy_size - 1))
        core = gx & (CORES - 1)
        low_first = ((within & 15) * BLOCK).astype(F32)
        high = (core * (rows_dev // LANES) + lax.shift_right_logical(within, 4)).astype(F32)
        chip = chip.astype(F32)
        so_far = jnp.dot(spread, up_to, preferred_element_type=F32)
        so_far = [so_far[:, r * LANES : (r + 1) * LANES] for r in range(BLOCK)]
        mine = lane_f == chip
        counted = jnp.where(mine, so_far[-1], 0.0)
        before = jnp.dot(earlier, counted.astype(BF16), preferred_element_type=F32) + total
        start = jnp.sum(jnp.where(mine, before, 0.0), axis=1, keepdims=True)
        total = total + jnp.sum(counted, axis=0, keepdims=True)
        depth = lane_f - start
        which = jnp.zeros((LANES, LANES), F32)
        for m in so_far:
            which = which + jnp.where(m <= depth, 1.0, 0.0)
        hit = (depth >= 0.0) & (depth < so_far[-1])
        both = jnp.concatenate(
            [jnp.where(hit, low_first + which, 0.0), jnp.where(hit, high, 0.0)], axis=1
        ).astype(BF16)
        chip_row = jnp.sum(jnp.where(diagonal, chip, 0.0), axis=0, keepdims=True)
        to_chip = jnp.where(sub.astype(F32) == chip_row, 1.0, 0.0).astype(BF16)
        low_high = low_high + jnp.dot(to_chip, both, preferred_element_type=F32)
        here = pl.ds(a * LANES, LANES)
        spreads[here, :] = spread
        starts[here, :] = jnp.broadcast_to(start, (LANES, LANES))
        chips[here, :] = jnp.broadcast_to(chip, (LANES, LANES))
    most = jnp.max(total, axis=1, keepdims=True)
    mark = jnp.where(most > CHIP_ROOM, float(MARK), 0.0)
    query = (low_high[:, :LANES] + low_high[:, LANES:] * float(LANES) + mark).astype(jnp.int32)
    for core in range(CORES):
        shares = pltpu.roll(query, LANES - core * ROOM, 1) if core else query
        for o in range(shards // CORES):
            device = (o // gy_size * CORES + core) * gy_size + o % gy_size
            queries[device] = shares[o : o + 1, :]

    piece = min(512, rows_dev)
    mine_from = core_me * rows_dev
    theirs_from = (CORES - 1 - core_me) * rows_dev

    def widen(source, start, j, carry):
        at = j * piece
        block = source[pl.ds(pl.multiple_of(at, piece), piece), :]
        wide[pl.ds(pl.multiple_of(start + at, piece), piece), :] = block.astype(F32)
        return carry

    for c in range(parts):
        load(c).wait()
    lax.fori_loop(0, rows_dev // piece, functools.partial(widen, packed, mine_from), 0)

    pl.semaphore_wait(barrier, shards - 1)
    shifted = shift_from(me, gy_size)
    twin = shifted(RING * RING)
    lend = send(table, twin_packed, table_send, table_recv, twin, gy_size)
    exchange_rows(queries, asked, me, shards, gy_size, ask_send, ask_recv)
    lend.start()
    own_ask = pltpu.make_async_copy(queries.at[me], asked.at[me], own_sem.at[1])
    own_ask.start()

    slab = min(2048, rows_dev)

    def step(j, gram):
        block = packed[pl.ds(pl.multiple_of(j * slab, slab), slab), :]
        return gram + lax.dot_general(
            block, block, (((0,), (0,)), ((), ())), preferred_element_type=F32
        )

    gram = lax.fori_loop(0, rows_dev // slab, step, jnp.zeros((LANES, LANES), F32))
    for o in range(LANES):
        terms[o] = gram[o : o + 1, :]
    exchange_rows(terms, arrived, me, shards, gy_size, term_send, term_recv)
    own_term = pltpu.make_async_copy(terms.at[me], arrived.at[me], own_sem.at[2])
    own_term.start()

    own_ask.wait()
    await_rows(asked, asked, shards, gy_size, ask_send, ask_recv)
    to_scalars = pltpu.make_async_copy(asked, asked_here, own_sem.at[3])
    to_scalars.start()
    lend.wait()
    lax.fori_loop(0, rows_dev // piece, functools.partial(widen, twin_packed, theirs_from), 0)
    to_scalars.wait()

    my_place = chip_me * CORES + core_me

    def collect(peer):
        for t in range(ROOM):
            row = asked_here[peer, 0, t] & (CORES * rows_dev - 1)
            stage[pl.ds(t, 1), :] = wide[pl.ds(row, 1), :]
        outgoing[peer] = stage[...].astype(BF16)

    def serve(i, carry):
        gx, gy = shifted(lax.rem(i * 77, shards))
        peer = gx * gy_size + gy
        collect(peer)
        send(outgoing.at[peer], landed.at[my_place], send_sem, recv_sem, (gx, gy), gy_size).start()
        return carry

    lax.fori_loop(1, SECOND, serve, 0)
    own_term.wait()
    await_rows(terms, arrived, shards, gy_size, term_send, term_recv)
    row_total[...] = jnp.sum(arrived[...], axis=0)

    def share(i, carry):
        peer = lax.rem(me + i, shards)
        send(row_total, gramian.at[me], sum_send, sum_recv, peer, gy_size).start()
        return carry

    lax.fori_loop(1, shards, share, 0)
    own_sum = pltpu.make_async_copy(row_total, gramian.at[me], own_sem.at[4])
    own_sum.start()
    lax.fori_loop(SECOND, shards, serve, 0)
    collect(me)
    own = pltpu.make_async_copy(outgoing.at[me], landed.at[my_place], own_sem.at[5])
    own.start()

    pos_chip = jnp.zeros((users, 2 * LANES), F32)
    for a in range(requests // LANES):
        here = pl.ds(a * LANES, LANES)
        back = lax.shift_right_logical(lane, bits(USER_BLOCKS)) + a * group == sub
        spread = spreads[here, :]
        live = spread.astype(F32) > 0.0
        spot = jnp.dot(spread, before_row, preferred_element_type=F32) + starts[here, :]
        both = jnp.concatenate(
            [jnp.where(live, spot, 0.0), jnp.where(live, chips[here, :], 0.0)], axis=1
        ).astype(BF16)
        back = jnp.where(back, 1.0, 0.0).astype(BF16)
        pos_chip = pos_chip + jnp.dot(back, both, preferred_element_type=F32)
    spot = pos_chip[:, :LANES] + pos_chip[:, LANES:] * float(CHIP_ROOM)
    spots_now = jnp.zeros((users, USER_ITEMS), F32)
    for item in range(USER_ITEMS):
        chosen = jnp.where(lane == row_index[:, item : item + 1], spot, 0.0)
        chosen = jnp.sum(chosen, axis=1, keepdims=True)
        spots_now = jnp.where(slot_lane == item, chosen, spots_now)
    spots[...] = spots_now.astype(jnp.int32)
    top[...] = jnp.max(jnp.max(asked[...], axis=0), axis=1, keepdims=True)

    spots_to = pltpu.make_async_copy(spots, spots_here, own_sem.at[0])
    spots_to.start()

    own_sum.wait()
    own.wait()
    await_rows(terms, gramian, shards, gy_size, sum_send, sum_recv)
    spots_to.wait()
    await_rows(outgoing, landed, shards, gy_size, send_sem, recv_sem)

    def widen_landed(j, carry):
        for t in range(8):
            at = pl.ds(pl.multiple_of((j * 8 + t) * ROOM, ROOM), ROOM)
            wide[at, :] = landed[j * 8 + t].astype(F32)
        return carry

    lax.fori_loop(0, shards // 8, widen_landed, 0)

    def take(user, carry):
        for item in range(USER_ITEMS):
            spot = spots_here[user, item] & (CORES * rows_dev - 1)
            rows[pl.ds(item * users + user, 1), :] = wide[pl.ds(spot, 1), :]
        return carry

    lax.fori_loop(0, users, take, 0)
    whole = jnp.concatenate([gramian[o] for o in range(LANES)], axis=0)
    conjugate(unobserved, whole, confidence, counts, out, rows, vectors, weights)


def solve_kernel(
    unobserved, spots, landed, gramian, confidence, counts, out, packed, wide, rows, vectors, weights, sem
):
    users = confidence.shape[1]
    parts = 8
    part = landed.shape[0] // parts

    def load(c):
        here = pl.ds(c * part, part)
        return pltpu.make_async_copy(landed.at[here], packed.at[here], sem.at[c])

    for c in range(parts):
        load(c).start()
    for c in range(parts):
        load(c).wait()
        here = pl.ds(c * part, part)
        wide[here, :] = packed[here, :].astype(F32)

    def pick(user, carry):
        for item in range(USER_ITEMS):
            rows[pl.ds(item * users + user, 1), :] = wide[pl.ds(spots[user, item], 1), :]
        return carry

    lax.fori_loop(0, users, pick, 0)
    conjugate(unobserved, gramian[...], confidence, counts, out, rows, vectors, weights)


def vmem():
    return pl.BlockSpec(memory_space=pltpu.VMEM)


def smem():
    return pl.BlockSpec(memory_space=pltpu.SMEM)


def anywhere():
    return pl.BlockSpec(memory_space=pl.ANY)


def ask(shards, gy_size, blocks_dev, ids, owner_map, need):
    requests = need.shape[0]
    dma = pltpu.SemaphoreType.DMA
    return pl.pallas_call(
        functools.partial(ask_kernel, shards, gy_size, blocks_dev),
        out_shape=(
            jax.ShapeDtypeStruct((shards, 1, LANES), jnp.int32),
            jax.ShapeDtypeStruct((requests, BLOCK), jnp.int32),
            jax.ShapeDtypeStruct((1, 1), jnp.int32),
        ),
        in_specs=[smem(), anywhere(), vmem()],
        out_specs=(vmem(), vmem(), vmem()),
        scratch_shapes=[
            pltpu.VMEM(owner_map.shape, jnp.int32),
            pltpu.VMEM((requests, LANES), jnp.int32),
            pltpu.VMEM((shards, 1, LANES), jnp.int32),
            dma, dma, dma, dma,
        ],
        compiler_params=pltpu.CompilerParams(
            collective_id=1, has_side_effects=True, vmem_limit_bytes=VMEM_LIMIT
        ),
        name="ask",
    )(ids, owner_map, need)


def fetch(shards, gy_size, room, asked, table):
    dma = pltpu.SemaphoreType.DMA
    return pl.pallas_call(
        functools.partial(fetch_kernel, shards, gy_size, room),
        out_shape=(
            jax.ShapeDtypeStruct((shards, room, LANES), BF16),
            jax.ShapeDtypeStruct((shards, 1, LANES), F32),
        ),
        in_specs=[smem(), anywhere()],
        out_specs=(anywhere(), vmem()),
        scratch_shapes=[
            pltpu.VMEM(table.shape, BF16),
            pltpu.VMEM(table.shape, F32),
            pltpu.VMEM((room, LANES), F32),
            pltpu.VMEM((shards, room, LANES), BF16),
            pltpu.VMEM((shards, 1, LANES), F32),
            pltpu.VMEM((shards, 1, LANES), F32),
            pltpu.VMEM((1, LANES), F32),
            pltpu.SemaphoreType.DMA((8,)),
            pltpu.SemaphoreType.DMA((3,)),
            dma, dma, dma, dma, dma, dma,
        ],
        compiler_params=pltpu.CompilerParams(
            collective_id=2,
            has_side_effects=True,
            vmem_limit_bytes=VMEM_LIMIT,
        ),
        name="fetch",
    )(asked, table)


def gather(
    shards, gy_size, blocks_dev, unobserved, block_ids, owner_map, slots, offsets, counts, confidence, table
):
    dma = pltpu.SemaphoreType.DMA
    users = slots.shape[1]
    line = (shards, 1, LANES)
    return pl.pallas_call(
        functools.partial(gather_kernel, shards, gy_size, blocks_dev, unobserved),
        out_shape=(
            jax.ShapeDtypeStruct((users, LANES), F32),
            jax.ShapeDtypeStruct((1, 1), jnp.int32),
        ),
        in_specs=[smem(), vmem(), anywhere(), vmem(), vmem(), vmem(), vmem(), anywhere()],
        out_specs=(vmem(), vmem()),
        scratch_shapes=[
            pltpu.VMEM(owner_map.shape, jnp.int32),
            pltpu.VMEM((users * USER_BLOCKS, LANES), jnp.int32),
            pltpu.VMEM(line, jnp.int32),
            pltpu.VMEM(line, jnp.int32),
            pltpu.SMEM(line, jnp.int32),
            pltpu.VMEM(table.shape, BF16),
            pltpu.VMEM(table.shape, BF16),
            pltpu.VMEM((CORES * table.shape[0], LANES), F32),
            pltpu.VMEM((ROOM, LANES), F32),
            pltpu.VMEM((shards, ROOM, LANES), BF16),
            pltpu.VMEM(line, F32),
            pltpu.VMEM(line, F32),
            pltpu.VMEM((1, LANES), F32),
            pltpu.VMEM((users * USER_BLOCKS, LANES), BF16),
            pltpu.VMEM((users * USER_BLOCKS, LANES), F32),
            pltpu.VMEM((users * USER_BLOCKS, LANES), F32),
            pltpu.VMEM((shards, ROOM, LANES), BF16),
            pltpu.VMEM(line, F32),
            pltpu.VMEM((users, USER_ITEMS), jnp.int32),
            pltpu.SMEM((users, USER_ITEMS), jnp.int32),
            pltpu.VMEM((USER_ITEMS * users, LANES), F32),
            pltpu.VMEM((USER_ITEMS, LANES, users), F32),
            pltpu.VMEM((USER_ITEMS, users), F32),
            pltpu.SemaphoreType.DMA((8,)),
            pltpu.SemaphoreType.DMA((6,)),
            dma, dma, dma, dma, dma, dma, dma, dma, dma, dma,
        ],
        compiler_params=pltpu.CompilerParams(
            collective_id=0, has_side_effects=True, vmem_limit_bytes=VMEM_LIMIT
        ),
        name="gather",
    )(block_ids, block_ids, owner_map, slots, offsets, counts, confidence, table)


def solve(unobserved, spots, landed, gramian, confidence, counts):
    users = confidence.shape[1]
    return pl.pallas_call(
        functools.partial(solve_kernel, unobserved),
        out_shape=jax.ShapeDtypeStruct((users, LANES), F32),
        in_specs=[smem(), anywhere(), vmem(), vmem(), vmem()],
        out_specs=vmem(),
        scratch_shapes=[
            pltpu.VMEM(landed.shape, BF16),
            pltpu.VMEM(landed.shape, F32),
            pltpu.VMEM((USER_ITEMS * users, LANES), F32),
            pltpu.VMEM((USER_ITEMS, LANES, users), F32),
            pltpu.VMEM((USER_ITEMS, users), F32),
            pltpu.SemaphoreType.DMA((8,)),
        ],
        compiler_params=pltpu.CompilerParams(vmem_limit_bytes=VMEM_LIMIT),
        name="solve",
    )(spots, landed, gramian, confidence, counts)


def fetch_all(shards, gy_size, blocks_dev, item_table, block_ids, item_slots, item_offsets, item_counts, owner_map):
    users = block_ids.shape[0]
    live = jnp.arange(USER_ITEMS)[None, :] < item_counts[:, None]
    row_index = item_slots * BLOCK + item_offsets
    candidates = jnp.arange(USER_BLOCKS * BLOCK, dtype=jnp.int32)
    hits = row_index[:, :, None] == candidates[None, None, :]
    need = jnp.any(hits & live[:, :, None], axis=1).astype(F32)
    asked, keys, _ = ask(
        shards,
        gy_size,
        blocks_dev,
        block_ids.reshape(-1, LANES),
        owner_map,
        need.reshape(users * USER_BLOCKS, BLOCK),
    )
    keys = keys.reshape(users, 1, USER_BLOCKS * BLOCK)
    spots = jnp.sum(jnp.where(hits, keys, 0), axis=2)
    landed, gramian = fetch(shards, gy_size, MOST, asked.reshape(shards, LANES), item_table)
    return spots, landed, gramian


def per_device(item_table, block_ids, item_slots, item_offsets, confidence, item_counts, owner_map):
    shards, gy_size = lax.axis_size(("gx", "gy")), lax.axis_size("gy")
    rows_dev = item_table.shape[0]
    blocks_dev = rows_dev // BLOCK
    users = block_ids.shape[0]
    unobserved = USER_ITEMS / (rows_dev * shards)
    owner_map = owner_map.reshape(-1, LANES)
    counts = item_counts.reshape(1, users)

    def finish(spots, landed, gramian):
        landed = landed.reshape(-1, LANES)
        gramian = gramian.reshape(LANES, LANES)
        return solve(unobserved, spots, landed, gramian, confidence.T, counts)

    factors, top = gather(
        shards, gy_size, blocks_dev, unobserved, block_ids.T, owner_map,
        item_slots.T, item_offsets.T, counts, confidence.T, item_table,
    )
    return lax.cond(
        top[0, 0] >= MARK,
        lambda: finish(
            *fetch_all(
                shards, gy_size, blocks_dev, item_table, block_ids,
                item_slots, item_offsets, item_counts, owner_map,
            )
        ),
        lambda: factors,
    )


def solution(mesh):
    return jax.shard_map(
        per_device,
        mesh=mesh,
        in_specs=(
            P(("gx", "gy"), None),
            P(("gx", "gy"), None),
            P(("gx", "gy"), None),
            P(("gx", "gy"), None),
            P(("gx", "gy"), None),
            P(("gx", "gy")),
            P(),
        ),
        out_specs=P(("gx", "gy"), None),
        check_vma=False,
    )
```

```python
import functools

import jax
import jax.numpy as jnp
from jax import lax
from jax.experimental import pallas as pl
from jax.experimental.pallas import tpu as pltpu
from jax.sharding import PartitionSpec as P

BLOCK = 8
USER_BLOCKS = 8
USER_ITEMS = 32
ITERATIONS = 16
LANES = 128
CORES = 2
RING = 4
ROOM = 48
CHIP_ROOM = CORES * ROOM
MOST = 128
MARK = 1 << 20

SECOND = 64

MESH = pl.DeviceIdType.MESH
F32 = jnp.float32
BF16 = jnp.bfloat16
VMEM_LIMIT = 56 * 1024 * 1024


def place(gy_size):
    gx, gy = lax.axis_index("gx"), lax.axis_index("gy")
    return gx * gy_size + gy


def signal_all(me, shards, gy_size):
    barrier = pltpu.get_barrier_semaphore()

    def one(i, carry):
        peer = lax.rem(me + i, shards)
        pl.semaphore_signal(
            barrier,
            inc=1,
            device_id=(peer // gy_size, lax.rem(peer, gy_size)),
            device_id_type=MESH,
        )
        return carry

    lax.fori_loop(1, shards, one, 0)
    return barrier


def send(src, dst, send_sem, recv_sem, peer, gy_size):
    return pltpu.make_async_remote_copy(
        src_ref=src,
        dst_ref=dst,
        send_sem=send_sem,
        recv_sem=recv_sem,
        device_id=peer if isinstance(peer, tuple) else (peer // gy_size, lax.rem(peer, gy_size)),
        device_id_type=MESH,
    )


def exchange_rows(table, landing, me, shards, gy_size, send_sem, recv_sem):
    def one(i, carry):
        peer = lax.rem(me + i, shards)
        send(table.at[peer], landing.at[me], send_sem, recv_sem, peer, gy_size).start()
        return carry

    lax.fori_loop(1, shards, one, 0)


def await_rows(table, landing, shards, gy_size, send_sem, recv_sem):
    others = pl.ds(0, shards - 1)
    send(table.at[others], landing.at[others], send_sem, recv_sem, 0, gy_size).wait()


def ask_kernel(
    shards, gy_size, blocks_dev, ids, owner_map, need, asked, keys, top,
    owners, found, queries, map_sem, own_sem, send_sem, recv_sem,
):
    me = place(gy_size)
    barrier = signal_all(me, shards, gy_size)
    load = pltpu.make_async_copy(owner_map, owners, map_sem)
    load.start()
    requests = found.shape[0]
    lane_row = lax.broadcasted_iota(jnp.int32, (1, LANES), 1)
    load.wait()

    def look(j, carry):
        for t in range(8):
            i = j * 8 + t
            block = ids[i // LANES, lax.rem(i, LANES)]
            row = owners[pl.ds(lax.shift_right_logical(block, 7), 1), :]
            found[pl.ds(i, 1), :] = jnp.where(lane_row == (block & (LANES - 1)), row, 0)
        return carry

    lax.fori_loop(0, requests // 8, look, 0)

    chunk = LANES
    lane = lax.broadcasted_iota(jnp.int32, (chunk, LANES), 1)
    sub = lax.broadcasted_iota(jnp.int32, (chunk, LANES), 0)
    lane8 = lax.broadcasted_iota(jnp.int32, (chunk, BLOCK), 1)
    earlier = jnp.where(lane < sub, 1.0, 0.0).astype(BF16)
    total = jnp.zeros((1, LANES), F32)
    low = jnp.zeros((LANES, LANES), F32)
    high = jnp.zeros((LANES, LANES), F32)
    over_rows = (((0,), (0,)), ((), ()))
    for a in range(requests // chunk):
        rows = pl.ds(a * chunk, chunk)
        storage = jnp.sum(found[rows, :].astype(F32), axis=1, keepdims=True).astype(jnp.int32)
        owner = storage // blocks_dev
        within = storage - owner * blocks_dev
        wanted = need[rows, :]
        count = jnp.sum(wanted, axis=1, keepdims=True)
        mine = owner == lane
        one_hot = jnp.where(mine, 1.0, 0.0).astype(BF16)
        counted = jnp.where(mine, count, 0.0)
        before = jnp.dot(earlier, counted.astype(BF16), preferred_element_type=F32) + total
        start = jnp.sum(jnp.where(mine, before, 0.0), axis=1, keepdims=True).astype(jnp.int32)
        total = total + jnp.sum(counted, axis=0, keepdims=True)
        first = within * BLOCK
        low_here = jnp.zeros((chunk, LANES), F32)
        high_here = jnp.zeros((chunk, LANES), F32)
        key = jnp.zeros((chunk, BLOCK), jnp.int32)
        for r in range(BLOCK):
            live = wanted[:, r : r + 1]
            row = first + r
            hit = jnp.where(lane == start, live, 0.0)
            low_here = low_here + hit * (row & (LANES - 1)).astype(F32)
            high_here = high_here + hit * lax.shift_right_logical(row, 7).astype(F32)
            spot = jnp.where(live > 0.0, owner * MOST + start, 0)
            key = jnp.where(lane8 == r, spot, key)
            start = start + live.astype(jnp.int32)
        keys[rows, :] = key
        low = low + lax.dot_general(
            one_hot, low_here.astype(BF16), over_rows, preferred_element_type=F32
        )
        high = high + lax.dot_general(
            one_hot, high_here.astype(BF16), over_rows, preferred_element_type=F32
        )
    most = jnp.max(total, axis=1, keepdims=True)
    mark = jnp.where(most > MOST, float(MARK), 0.0)
    query = (low + high * float(LANES) + mark).astype(jnp.int32)
    for o in range(shards):
        queries[o] = query[o : o + 1, :]

    pl.semaphore_wait(barrier, shards - 1)
    exchange_rows(queries, asked, me, shards, gy_size, send_sem, recv_sem)
    own = pltpu.make_async_copy(queries.at[me], asked.at[me], own_sem)
    own.start()
    own.wait()
    await_rows(queries, asked, shards, gy_size, send_sem, recv_sem)
    top[...] = jnp.max(jnp.max(asked[...], axis=0), axis=1, keepdims=True)


def fetch_kernel(
    shards, gy_size, room, asked, table, landed, gramian,
    packed, wide, stage, outgoing, terms, arrived, row_total, table_sem, own_sem,
    send_sem, recv_sem, term_send, term_recv, sum_send, sum_recv,
):
    me = place(gy_size)
    barrier = signal_all(me, shards, gy_size)
    rows_dev = table.shape[0]
    parts = 8
    part = rows_dev // parts

    def load(c):
        rows = pl.ds(c * part, part)
        return pltpu.make_async_copy(table.at[rows], packed.at[rows], table_sem.at[c])

    for c in range(parts):
        load(c).start()
    piece = min(512, part)
    total = jnp.zeros((LANES, LANES), F32)
    for c in range(parts):
        load(c).wait()

        def step(j, total):
            rows = pl.ds(pl.multiple_of(c * part + j * piece, piece), piece)
            block = packed[rows, :]
            wide[rows, :] = block.astype(F32)
            return total + lax.dot_general(
                block, block, (((0,), (0,)), ((), ())), preferred_element_type=F32
            )

        total = lax.fori_loop(0, part // piece, step, total)
    for o in range(shards):
        terms[o] = total[o : o + 1, :]

    pl.semaphore_wait(barrier, shards - 1)
    exchange_rows(terms, arrived, me, shards, gy_size, term_send, term_recv)
    own_term = pltpu.make_async_copy(terms.at[me], arrived.at[me], own_sem.at[0])
    own_term.start()

    def collect(peer):
        for h in range(room // 16):
            for t in range(16):
                row = asked[peer, h * 16 + t] & (rows_dev - 1)
                stage[pl.ds(h * 16 + t, 1), :] = wide[pl.ds(row, 1), :]
        outgoing[peer] = stage[...].astype(BF16)

    def serve(i, carry):
        off = lax.rem(i * 77, shards)
        peer = lax.rem(me + off, shards)
        collect(peer)
        send(outgoing.at[peer], landed.at[me], send_sem, recv_sem, peer, gy_size).start()
        return carry

    lax.fori_loop(1, shards // 2, serve, 0)
    own_term.wait()
    await_rows(terms, arrived, shards, gy_size, term_send, term_recv)
    row_total[...] = jnp.sum(arrived[...], axis=0)

    def share(i, carry):
        peer = lax.rem(me + i, shards)
        send(row_total, gramian.at[me], sum_send, sum_recv, peer, gy_size).start()
        return carry

    lax.fori_loop(1, shards, share, 0)
    own_sum = pltpu.make_async_copy(row_total, gramian.at[me], own_sem.at[1])
    own_sum.start()
    lax.fori_loop(shards // 2, shards, serve, 0)
    collect(me)
    own = pltpu.make_async_copy(outgoing.at[me], landed.at[me], own_sem.at[2])
    own.start()
    own_sum.wait()
    own.wait()
    await_rows(terms, gramian, shards, gy_size, sum_send, sum_recv)
    await_rows(outgoing, landed, shards, gy_size, send_sem, recv_sem)


def bits(count):
    assert count & (count - 1) == 0
    return count.bit_length() - 1


def chip_of(device, gy_size):
    gx, gy = device // gy_size, lax.rem(device, gy_size)
    return (gx // CORES) * gy_size + gy, lax.rem(gx, CORES)


def shift_from(me, gy_size):
    gx, gy = me // gy_size, lax.rem(me, gy_size)
    y, core, x, z = gx // CORES, lax.rem(gx, CORES), gy // RING, lax.rem(gy, RING)

    def shifted(off):
        gx = lax.rem(y + off // (RING * RING * CORES), RING) * CORES
        gx = gx + lax.rem(core + off // (RING * RING), CORES)
        return gx, lax.rem(x + off // RING, RING) * RING + lax.rem(z + off, RING)

    return shifted


def conjugate(unobserved, gramian, confidence, counts, out, rows, vectors, weights):
    users = confidence.shape[1]
    unit = jnp.where(
        lax.broadcasted_iota(jnp.int32, (LANES, LANES), 0)
        == lax.broadcasted_iota(jnp.int32, (LANES, LANES), 1),
        1.0,
        0.0,
    ).astype(BF16)
    for item in range(USER_ITEMS):
        block = rows[pl.ds(item * users, users), :].astype(BF16)
        vectors[item] = lax.dot_general(
            unit, block, (((1,), (1,)), ((), ())), preferred_element_type=F32
        )

    item_sub = lax.broadcasted_iota(jnp.int32, (USER_ITEMS, users), 0)
    weights[...] = jnp.where(item_sub < counts[...], confidence[...], 0.0)
    scaled = gramian * unobserved
    top = scaled.astype(BF16)
    rest = (scaled - top.astype(F32)).astype(BF16)

    right = jnp.zeros((LANES, users), F32)
    for item in range(USER_ITEMS):
        right = right + vectors[item] * weights[item : item + 1, :]
    norm = jnp.sum(right * right, axis=0, keepdims=True)

    def sweep(_, carry):
        solution, residual, direction, norm = carry
        d_top = direction.astype(BF16)
        d_rest = (direction - d_top.astype(F32)).astype(BF16)
        image = direction
        unobserved_part = (
            jnp.dot(top, d_top, preferred_element_type=F32)
            + jnp.dot(top, d_rest, preferred_element_type=F32)
            + jnp.dot(rest, d_top, preferred_element_type=F32)
        )
        for item in range(USER_ITEMS):
            vector = vectors[item]
            projected = jnp.sum(vector * direction, axis=0, keepdims=True)
            image = image + vector * (weights[item : item + 1, :] * projected)
        image = image + unobserved_part
        alpha = norm / jnp.sum(direction * image, axis=0, keepdims=True)
        solution = solution + alpha * direction
        residual = residual - alpha * image
        after = jnp.sum(residual * residual, axis=0, keepdims=True)
        direction = residual + (after / norm) * direction
        return solution, residual, direction, after

    solution, *_ = lax.fori_loop(
        0, ITERATIONS, sweep, (jnp.zeros_like(right), right, right, norm)
    )
    out[...] = solution.T


def gather_kernel(
    shards, gy_size, blocks_dev, unobserved,
    ids, id_rows, owner_map, slots, offsets, counts, confidence, table, out, top,
    owners, found, queries, asked, asked_here, packed, twin_packed, wide, stage, outgoing,
    terms, arrived, row_total, spreads, starts, chips,
    landed, gramian, spots, spots_here, rows, vectors, weights, load_sem, own_sem, table_send, table_recv,
    send_sem, recv_sem, ask_send, ask_recv, term_send, term_recv, sum_send, sum_recv,
):
    me = place(gy_size)
    chip_me, core_me = chip_of(me, gy_size)
    barrier = signal_all(me, shards, gy_size)
    load_map = pltpu.make_async_copy(owner_map, owners, own_sem.at[0])
    load_map.start()
    rows_dev = table.shape[0]
    parts = 8
    part = rows_dev // parts

    def load(c):
        rows = pl.ds(c * part, part)
        return pltpu.make_async_copy(table.at[rows], packed.at[rows], load_sem.at[c])

    for c in range(parts):
        load(c).start()

    users = slots.shape[1]
    requests = found.shape[0]
    group = LANES // USER_BLOCKS
    lane = lax.broadcasted_iota(jnp.int32, (LANES, LANES), 1)
    sub = lax.broadcasted_iota(jnp.int32, (LANES, LANES), 0)
    lane_f = lane.astype(F32)
    diagonal = lane == sub

    item_sub = lax.broadcasted_iota(jnp.int32, (USER_ITEMS, users), 0)
    slot_lane = lax.broadcasted_iota(jnp.int32, (users, USER_ITEMS), 1)
    row_index = slots[...] * BLOCK + offsets[...]
    row_index = jnp.where(item_sub < counts[...], row_index, -1).astype(F32)
    inner = (id_rows[...] & (LANES - 1)).astype(F32)
    by_user = jnp.concatenate(
        [row_index, inner, jnp.zeros((LANES - USER_ITEMS - USER_BLOCKS, users), F32)], axis=0
    ).T
    row_index = by_user[:, :USER_ITEMS].astype(jnp.int32)
    inner = by_user.astype(BF16)
    wanted = lane == row_index[:, 0:1]
    for item in range(1, USER_ITEMS):
        wanted = wanted | (lane == row_index[:, item : item + 1])
    wanted = jnp.where(wanted, 1.0, 0.0).astype(BF16)
    wanted_inner = jnp.concatenate([wanted, inner], axis=1)

    load_map.wait()

    def look(user, carry):
        for slot in range(USER_BLOCKS):
            line = lax.shift_right_logical(ids[slot, user], bits(LANES))
            found[pl.ds(user * USER_BLOCKS + slot, 1), :] = owners[pl.ds(line, 1), :]
        return carry

    lax.fori_loop(0, users, look, 0, unroll=2)

    same = lax.shift_right_logical(lane, 3) == (sub & 7)
    own_lane = lane == (sub & 7) + USER_ITEMS
    earlier = jnp.where(lane < sub, 1.0, 0.0).astype(BF16)
    before_row = jnp.where(
        (lax.shift_right_logical(lane, 3) == lax.shift_right_logical(sub, 3))
        & ((sub & 7) < (lane & 7)),
        1.0,
        0.0,
    ).astype(BF16)
    up_to = jnp.concatenate(
        [jnp.where((sub & 7) <= r, 1.0, 0.0).astype(BF16) for r in range(BLOCK)], axis=1
    )
    total = jnp.zeros((1, LANES), F32)
    low_high = jnp.zeros((LANES, 2 * LANES), F32)
    for a in range(requests // LANES):
        pick = jnp.where(lax.shift_right_logical(sub, bits(USER_BLOCKS)) + a * group == lane, 1.0, 0.0).astype(BF16)
        picked = jnp.dot(pick, wanted_inner, preferred_element_type=F32)
        spread = jnp.where(same, picked[:, :LANES], 0.0).astype(BF16)
        inner_here = jnp.sum(jnp.where(own_lane, picked[:, LANES:], 0.0), axis=1, keepdims=True)
        line = found[pl.ds(a * LANES, LANES), :].astype(F32)
        storage = jnp.sum(jnp.where(lane_f == inner_here, line, 0.0), axis=1, keepdims=True)
        storage = storage.astype(jnp.int32)
        device = lax.shift_right_logical(storage, bits(blocks_dev))
        within = storage & (blocks_dev - 1)
        gx = lax.shift_right_logical(device, bits(gy_size))
        chip = lax.shift_right_logical(gx, bits(CORES)) * gy_size + (device & (gy_size - 1))
        core = gx & (CORES - 1)
        low_first = ((within & 15) * BLOCK).astype(F32)
        high = (core * (rows_dev // LANES) + lax.shift_right_logical(within, 4)).astype(F32)
        chip = chip.astype(F32)
        so_far = jnp.dot(spread, up_to, preferred_element_type=F32)
        so_far = [so_far[:, r * LANES : (r + 1) * LANES] for r in range(BLOCK)]
        mine = lane_f == chip
        counted = jnp.where(mine, so_far[-1], 0.0)
        before = jnp.dot(earlier, counted.astype(BF16), preferred_element_type=F32) + total
        start = jnp.sum(jnp.where(mine, before, 0.0), axis=1, keepdims=True)
        total = total + jnp.sum(counted, axis=0, keepdims=True)
        depth = lane_f - start
        which = jnp.zeros((LANES, LANES), F32)
        for m in so_far:
            which = which + jnp.where(m <= depth, 1.0, 0.0)
        hit = (depth >= 0.0) & (depth < so_far[-1])
        both = jnp.concatenate(
            [jnp.where(hit, low_first + which, 0.0), jnp.where(hit, high, 0.0)], axis=1
        ).astype(BF16)
        chip_row = jnp.sum(jnp.where(diagonal, chip, 0.0), axis=0, keepdims=True)
        to_chip = jnp.where(sub.astype(F32) == chip_row, 1.0, 0.0).astype(BF16)
        low_high = low_high + jnp.dot(to_chip, both, preferred_element_type=F32)
        here = pl.ds(a * LANES, LANES)
        spreads[here, :] = spread
        starts[here, :] = jnp.broadcast_to(start, (LANES, LANES))
        chips[here, :] = jnp.broadcast_to(chip, (LANES, LANES))
    most = jnp.max(total, axis=1, keepdims=True)
    mark = jnp.where(most > CHIP_ROOM, float(MARK), 0.0)
    query = (low_high[:, :LANES] + low_high[:, LANES:] * float(LANES) + mark).astype(jnp.int32)
    for core in range(CORES):
        shares = pltpu.roll(query, LANES - core * ROOM, 1) if core else query
        for o in range(shards // CORES):
            device = (o // gy_size * CORES + core) * gy_size + o % gy_size
            queries[device] = shares[o : o + 1, :]

    piece = min(512, rows_dev)
    mine_from = core_me * rows_dev
    theirs_from = (CORES - 1 - core_me) * rows_dev

    def widen(source, start, j, carry):
        at = j * piece
        block = source[pl.ds(pl.multiple_of(at, piece), piece), :]
        wide[pl.ds(pl.multiple_of(start + at, piece), piece), :] = block.astype(F32)
        return carry

    for c in range(parts):
        load(c).wait()
    lax.fori_loop(0, rows_dev // piece, functools.partial(widen, packed, mine_from), 0)

    pl.semaphore_wait(barrier, shards - 1)
    shifted = shift_from(me, gy_size)
    twin = shifted(RING * RING)
    lend = send(table, twin_packed, table_send, table_recv, twin, gy_size)
    exchange_rows(queries, asked, me, shards, gy_size, ask_send, ask_recv)
    lend.start()
    own_ask = pltpu.make_async_copy(queries.at[me], asked.at[me], own_sem.at[1])
    own_ask.start()

    slab = min(2048, rows_dev)

    def step(j, gram):
        block = packed[pl.ds(pl.multiple_of(j * slab, slab), slab), :]
        return gram + lax.dot_general(
            block, block, (((0,), (0,)), ((), ())), preferred_element_type=F32
        )

    gram = lax.fori_loop(0, rows_dev // slab, step, jnp.zeros((LANES, LANES), F32))
    for o in range(LANES):
        terms[o] = gram[o : o + 1, :]
    exchange_rows(terms, arrived, me, shards, gy_size, term_send, term_recv)
    own_term = pltpu.make_async_copy(terms.at[me], arrived.at[me], own_sem.at[2])
    own_term.start()

    own_ask.wait()
    await_rows(asked, asked, shards, gy_size, ask_send, ask_recv)
    to_scalars = pltpu.make_async_copy(asked, asked_here, own_sem.at[3])
    to_scalars.start()
    lend.wait()
    lax.fori_loop(0, rows_dev // piece, functools.partial(widen, twin_packed, theirs_from), 0)
    to_scalars.wait()

    my_place = chip_me * CORES + core_me

    def collect(peer):
        for t in range(ROOM):
            row = asked_here[peer, 0, t] & (CORES * rows_dev - 1)
            stage[pl.ds(t, 1), :] = wide[pl.ds(row, 1), :]
        outgoing[peer] = stage[...].astype(BF16)

    def serve(i, carry):
        gx, gy = shifted(lax.rem(i * (77 - 26 * core_me), shards))
        peer = gx * gy_size + gy
        collect(peer)
        send(outgoing.at[peer], landed.at[my_place], send_sem, recv_sem, (gx, gy), gy_size).start()
        return carry

    lax.fori_loop(1, SECOND, serve, 0)
    own_term.wait()
    await_rows(terms, arrived, shards, gy_size, term_send, term_recv)
    row_total[...] = jnp.sum(arrived[...], axis=0)

    def share(i, carry):
        peer = lax.rem(me + i, shards)
        send(row_total, gramian.at[me], sum_send, sum_recv, peer, gy_size).start()
        return carry

    lax.fori_loop(1, shards, share, 0)
    own_sum = pltpu.make_async_copy(row_total, gramian.at[me], own_sem.at[4])
    own_sum.start()
    lax.fori_loop(SECOND, shards, serve, 0)
    collect(me)
    own = pltpu.make_async_copy(outgoing.at[me], landed.at[my_place], own_sem.at[5])
    own.start()

    pos_chip = jnp.zeros((users, 2 * LANES), F32)
    for a in range(requests // LANES):
        here = pl.ds(a * LANES, LANES)
        back = lax.shift_right_logical(lane, bits(USER_BLOCKS)) + a * group == sub
        spread = spreads[here, :]
        live = spread.astype(F32) > 0.0
        spot = jnp.dot(spread, before_row, preferred_element_type=F32) + starts[here, :]
        both = jnp.concatenate(
            [jnp.where(live, spot, 0.0), jnp.where(live, chips[here, :], 0.0)], axis=1
        ).astype(BF16)
        back = jnp.where(back, 1.0, 0.0).astype(BF16)
        pos_chip = pos_chip + jnp.dot(back, both, preferred_element_type=F32)
    spot = pos_chip[:, :LANES] + pos_chip[:, LANES:] * float(CHIP_ROOM)
    spots_now = jnp.zeros((users, USER_ITEMS), F32)
    for item in range(USER_ITEMS):
        chosen = jnp.where(lane == row_index[:, item : item + 1], spot, 0.0)
        chosen = jnp.sum(chosen, axis=1, keepdims=True)
        spots_now = jnp.where(slot_lane == item, chosen, spots_now)
    spots[...] = spots_now.astype(jnp.int32)
    top[...] = jnp.max(jnp.max(asked[...], axis=0), axis=1, keepdims=True)

    spots_to = pltpu.make_async_copy(spots, spots_here, own_sem.at[0])
    spots_to.start()

    own_sum.wait()
    own.wait()
    await_rows(terms, gramian, shards, gy_size, sum_send, sum_recv)
    spots_to.wait()
    await_rows(outgoing, landed, shards, gy_size, send_sem, recv_sem)

    def widen_landed(j, carry):
        for t in range(8):
            at = pl.ds(pl.multiple_of((j * 8 + t) * ROOM, ROOM), ROOM)
            wide[at, :] = landed[j * 8 + t].astype(F32)
        return carry

    lax.fori_loop(0, shards // 8, widen_landed, 0)

    def take(user, carry):
        for item in range(USER_ITEMS):
            spot = spots_here[user, item] & (CORES * rows_dev - 1)
            rows[pl.ds(item * users + user, 1), :] = wide[pl.ds(spot, 1), :]
        return carry

    lax.fori_loop(0, users, take, 0)
    whole = jnp.concatenate([gramian[o] for o in range(LANES)], axis=0)
    conjugate(unobserved, whole, confidence, counts, out, rows, vectors, weights)


def solve_kernel(
    unobserved, spots, landed, gramian, confidence, counts, out, packed, wide, rows, vectors, weights, sem
):
    users = confidence.shape[1]
    parts = 8
    part = landed.shape[0] // parts

    def load(c):
        here = pl.ds(c * part, part)
        return pltpu.make_async_copy(landed.at[here], packed.at[here], sem.at[c])

    for c in range(parts):
        load(c).start()
    for c in range(parts):
        load(c).wait()
        here = pl.ds(c * part, part)
        wide[here, :] = packed[here, :].astype(F32)

    def pick(user, carry):
        for item in range(USER_ITEMS):
            rows[pl.ds(item * users + user, 1), :] = wide[pl.ds(spots[user, item], 1), :]
        return carry

    lax.fori_loop(0, users, pick, 0)
    conjugate(unobserved, gramian[...], confidence, counts, out, rows, vectors, weights)


def vmem():
    return pl.BlockSpec(memory_space=pltpu.VMEM)


def smem():
    return pl.BlockSpec(memory_space=pltpu.SMEM)


def anywhere():
    return pl.BlockSpec(memory_space=pl.ANY)


def ask(shards, gy_size, blocks_dev, ids, owner_map, need):
    requests = need.shape[0]
    dma = pltpu.SemaphoreType.DMA
    return pl.pallas_call(
        functools.partial(ask_kernel, shards, gy_size, blocks_dev),
        out_shape=(
            jax.ShapeDtypeStruct((shards, 1, LANES), jnp.int32),
            jax.ShapeDtypeStruct((requests, BLOCK), jnp.int32),
            jax.ShapeDtypeStruct((1, 1), jnp.int32),
        ),
        in_specs=[smem(), anywhere(), vmem()],
        out_specs=(vmem(), vmem(), vmem()),
        scratch_shapes=[
            pltpu.VMEM(owner_map.shape, jnp.int32),
            pltpu.VMEM((requests, LANES), jnp.int32),
            pltpu.VMEM((shards, 1, LANES), jnp.int32),
            dma, dma, dma, dma,
        ],
        compiler_params=pltpu.CompilerParams(
            collective_id=1, has_side_effects=True, vmem_limit_bytes=VMEM_LIMIT
        ),
        name="ask",
    )(ids, owner_map, need)


def fetch(shards, gy_size, room, asked, table):
    dma = pltpu.SemaphoreType.DMA
    return pl.pallas_call(
        functools.partial(fetch_kernel, shards, gy_size, room),
        out_shape=(
            jax.ShapeDtypeStruct((shards, room, LANES), BF16),
            jax.ShapeDtypeStruct((shards, 1, LANES), F32),
        ),
        in_specs=[smem(), anywhere()],
        out_specs=(anywhere(), vmem()),
        scratch_shapes=[
            pltpu.VMEM(table.shape, BF16),
            pltpu.VMEM(table.shape, F32),
            pltpu.VMEM((room, LANES), F32),
            pltpu.VMEM((shards, room, LANES), BF16),
            pltpu.VMEM((shards, 1, LANES), F32),
            pltpu.VMEM((shards, 1, LANES), F32),
            pltpu.VMEM((1, LANES), F32),
            pltpu.SemaphoreType.DMA((8,)),
            pltpu.SemaphoreType.DMA((3,)),
            dma, dma, dma, dma, dma, dma,
        ],
        compiler_params=pltpu.CompilerParams(
            collective_id=2,
            has_side_effects=True,
            vmem_limit_bytes=VMEM_LIMIT,
        ),
        name="fetch",
    )(asked, table)


def gather(
    shards, gy_size, blocks_dev, unobserved, block_ids, owner_map, slots, offsets, counts, confidence, table
):
    dma = pltpu.SemaphoreType.DMA
    users = slots.shape[1]
    line = (shards, 1, LANES)
    return pl.pallas_call(
        functools.partial(gather_kernel, shards, gy_size, blocks_dev, unobserved),
        out_shape=(
            jax.ShapeDtypeStruct((users, LANES), F32),
            jax.ShapeDtypeStruct((1, 1), jnp.int32),
        ),
        in_specs=[smem(), vmem(), anywhere(), vmem(), vmem(), vmem(), vmem(), anywhere()],
        out_specs=(vmem(), vmem()),
        scratch_shapes=[
            pltpu.VMEM(owner_map.shape, jnp.int32),
            pltpu.VMEM((users * USER_BLOCKS, LANES), jnp.int32),
            pltpu.VMEM(line, jnp.int32),
            pltpu.VMEM(line, jnp.int32),
            pltpu.SMEM(line, jnp.int32),
            pltpu.VMEM(table.shape, BF16),
            pltpu.VMEM(table.shape, BF16),
            pltpu.VMEM((CORES * table.shape[0], LANES), F32),
            pltpu.VMEM((ROOM, LANES), F32),
            pltpu.VMEM((shards, ROOM, LANES), BF16),
            pltpu.VMEM(line, F32),
            pltpu.VMEM(line, F32),
            pltpu.VMEM((1, LANES), F32),
            pltpu.VMEM((users * USER_BLOCKS, LANES), BF16),
            pltpu.VMEM((users * USER_BLOCKS, LANES), F32),
            pltpu.VMEM((users * USER_BLOCKS, LANES), F32),
            pltpu.VMEM((shards, ROOM, LANES), BF16),
            pltpu.VMEM(line, F32),
            pltpu.VMEM((users, USER_ITEMS), jnp.int32),
            pltpu.SMEM((users, USER_ITEMS), jnp.int32),
            pltpu.VMEM((USER_ITEMS * users, LANES), F32),
            pltpu.VMEM((USER_ITEMS, LANES, users), F32),
            pltpu.VMEM((USER_ITEMS, users), F32),
            pltpu.SemaphoreType.DMA((8,)),
            pltpu.SemaphoreType.DMA((6,)),
            dma, dma, dma, dma, dma, dma, dma, dma, dma, dma,
        ],
        compiler_params=pltpu.CompilerParams(
            collective_id=0, has_side_effects=True, vmem_limit_bytes=VMEM_LIMIT
        ),
        name="gather",
    )(block_ids, block_ids, owner_map, slots, offsets, counts, confidence, table)


def solve(unobserved, spots, landed, gramian, confidence, counts):
    users = confidence.shape[1]
    return pl.pallas_call(
        functools.partial(solve_kernel, unobserved),
        out_shape=jax.ShapeDtypeStruct((users, LANES), F32),
        in_specs=[smem(), anywhere(), vmem(), vmem(), vmem()],
        out_specs=vmem(),
        scratch_shapes=[
            pltpu.VMEM(landed.shape, BF16),
            pltpu.VMEM(landed.shape, F32),
            pltpu.VMEM((USER_ITEMS * users, LANES), F32),
            pltpu.VMEM((USER_ITEMS, LANES, users), F32),
            pltpu.VMEM((USER_ITEMS, users), F32),
            pltpu.SemaphoreType.DMA((8,)),
        ],
        compiler_params=pltpu.CompilerParams(vmem_limit_bytes=VMEM_LIMIT),
        name="solve",
    )(spots, landed, gramian, confidence, counts)


def fetch_all(shards, gy_size, blocks_dev, item_table, block_ids, item_slots, item_offsets, item_counts, owner_map):
    users = block_ids.shape[0]
    live = jnp.arange(USER_ITEMS)[None, :] < item_counts[:, None]
    row_index = item_slots * BLOCK + item_offsets
    candidates = jnp.arange(USER_BLOCKS * BLOCK, dtype=jnp.int32)
    hits = row_index[:, :, None] == candidates[None, None, :]
    need = jnp.any(hits & live[:, :, None], axis=1).astype(F32)
    asked, keys, _ = ask(
        shards,
        gy_size,
        blocks_dev,
        block_ids.reshape(-1, LANES),
        owner_map,
        need.reshape(users * USER_BLOCKS, BLOCK),
    )
    keys = keys.reshape(users, 1, USER_BLOCKS * BLOCK)
    spots = jnp.sum(jnp.where(hits, keys, 0), axis=2)
    landed, gramian = fetch(shards, gy_size, MOST, asked.reshape(shards, LANES), item_table)
    return spots, landed, gramian


def per_device(item_table, block_ids, item_slots, item_offsets, confidence, item_counts, owner_map):
    shards, gy_size = lax.axis_size(("gx", "gy")), lax.axis_size("gy")
    rows_dev = item_table.shape[0]
    blocks_dev = rows_dev // BLOCK
    users = block_ids.shape[0]
    unobserved = USER_ITEMS / (rows_dev * shards)
    owner_map = owner_map.reshape(-1, LANES)
    counts = item_counts.reshape(1, users)

    def finish(spots, landed, gramian):
        landed = landed.reshape(-1, LANES)
        gramian = gramian.reshape(LANES, LANES)
        return solve(unobserved, spots, landed, gramian, confidence.T, counts)

    factors, top = gather(
        shards, gy_size, blocks_dev, unobserved, block_ids.T, owner_map,
        item_slots.T, item_offsets.T, counts, confidence.T, item_table,
    )
    return lax.cond(
        top[0, 0] >= MARK,
        lambda: finish(
            *fetch_all(
                shards, gy_size, blocks_dev, item_table, block_ids,
                item_slots, item_offsets, item_counts, owner_map,
            )
        ),
        lambda: factors,
    )


def solution(mesh):
    return jax.shard_map(
        per_device,
        mesh=mesh,
        in_specs=(
            P(("gx", "gy"), None),
            P(("gx", "gy"), None),
            P(("gx", "gy"), None),
            P(("gx", "gy"), None),
            P(("gx", "gy"), None),
            P(("gx", "gy")),
            P(),
        ),
        out_specs=P(("gx", "gy"), None),
        check_vma=False,
    )
```

```python
import functools

import jax
import jax.numpy as jnp
from jax import lax
from jax.experimental import pallas as pl
from jax.experimental.pallas import tpu as pltpu
from jax.sharding import PartitionSpec as P

BLOCK = 8
USER_BLOCKS = 8
USER_ITEMS = 32
ITERATIONS = 16
LANES = 128
CORES = 2
RING = 4
ROOM = 48
CHIP_ROOM = CORES * ROOM
MOST = 128
MARK = 1 << 20

SECOND = 64

MESH = pl.DeviceIdType.MESH
F32 = jnp.float32
BF16 = jnp.bfloat16
VMEM_LIMIT = 56 * 1024 * 1024


def place(gy_size):
    gx, gy = lax.axis_index("gx"), lax.axis_index("gy")
    return gx * gy_size + gy


def signal_all(me, shards, gy_size):
    barrier = pltpu.get_barrier_semaphore()

    def one(i, carry):
        peer = lax.rem(me + i, shards)
        pl.semaphore_signal(
            barrier,
            inc=1,
            device_id=(peer // gy_size, lax.rem(peer, gy_size)),
            device_id_type=MESH,
        )
        return carry

    lax.fori_loop(1, shards, one, 0)
    return barrier


def send(src, dst, send_sem, recv_sem, peer, gy_size):
    return pltpu.make_async_remote_copy(
        src_ref=src,
        dst_ref=dst,
        send_sem=send_sem,
        recv_sem=recv_sem,
        device_id=peer if isinstance(peer, tuple) else (peer // gy_size, lax.rem(peer, gy_size)),
        device_id_type=MESH,
    )


def exchange_rows(table, landing, me, shards, gy_size, send_sem, recv_sem):
    def one(i, carry):
        peer = lax.rem(me + i, shards)
        send(table.at[peer], landing.at[me], send_sem, recv_sem, peer, gy_size).start()
        return carry

    lax.fori_loop(1, shards, one, 0)


def await_rows(table, landing, shards, gy_size, send_sem, recv_sem):
    others = pl.ds(0, shards - 1)
    send(table.at[others], landing.at[others], send_sem, recv_sem, 0, gy_size).wait()


def ask_kernel(
    shards, gy_size, blocks_dev, ids, owner_map, need, asked, keys, top,
    owners, found, queries, map_sem, own_sem, send_sem, recv_sem,
):
    me = place(gy_size)
    barrier = signal_all(me, shards, gy_size)
    load = pltpu.make_async_copy(owner_map, owners, map_sem)
    load.start()
    requests = found.shape[0]
    lane_row = lax.broadcasted_iota(jnp.int32, (1, LANES), 1)
    load.wait()

    def look(j, carry):
        for t in range(8):
            i = j * 8 + t
            block = ids[i // LANES, lax.rem(i, LANES)]
            row = owners[pl.ds(lax.shift_right_logical(block, 7), 1), :]
            found[pl.ds(i, 1), :] = jnp.where(lane_row == (block & (LANES - 1)), row, 0)
        return carry

    lax.fori_loop(0, requests // 8, look, 0)

    chunk = LANES
    lane = lax.broadcasted_iota(jnp.int32, (chunk, LANES), 1)
    sub = lax.broadcasted_iota(jnp.int32, (chunk, LANES), 0)
    lane8 = lax.broadcasted_iota(jnp.int32, (chunk, BLOCK), 1)
    earlier = jnp.where(lane < sub, 1.0, 0.0).astype(BF16)
    total = jnp.zeros((1, LANES), F32)
    low = jnp.zeros((LANES, LANES), F32)
    high = jnp.zeros((LANES, LANES), F32)
    over_rows = (((0,), (0,)), ((), ()))
    for a in range(requests // chunk):
        rows = pl.ds(a * chunk, chunk)
        storage = jnp.sum(found[rows, :].astype(F32), axis=1, keepdims=True).astype(jnp.int32)
        owner = storage // blocks_dev
        within = storage - owner * blocks_dev
        wanted = need[rows, :]
        count = jnp.sum(wanted, axis=1, keepdims=True)
        mine = owner == lane
        one_hot = jnp.where(mine, 1.0, 0.0).astype(BF16)
        counted = jnp.where(mine, count, 0.0)
        before = jnp.dot(earlier, counted.astype(BF16), preferred_element_type=F32) + total
        start = jnp.sum(jnp.where(mine, before, 0.0), axis=1, keepdims=True).astype(jnp.int32)
        total = total + jnp.sum(counted, axis=0, keepdims=True)
        first = within * BLOCK
        low_here = jnp.zeros((chunk, LANES), F32)
        high_here = jnp.zeros((chunk, LANES), F32)
        key = jnp.zeros((chunk, BLOCK), jnp.int32)
        for r in range(BLOCK):
            live = wanted[:, r : r + 1]
            row = first + r
            hit = jnp.where(lane == start, live, 0.0)
            low_here = low_here + hit * (row & (LANES - 1)).astype(F32)
            high_here = high_here + hit * lax.shift_right_logical(row, 7).astype(F32)
            spot = jnp.where(live > 0.0, owner * MOST + start, 0)
            key = jnp.where(lane8 == r, spot, key)
            start = start + live.astype(jnp.int32)
        keys[rows, :] = key
        low = low + lax.dot_general(
            one_hot, low_here.astype(BF16), over_rows, preferred_element_type=F32
        )
        high = high + lax.dot_general(
            one_hot, high_here.astype(BF16), over_rows, preferred_element_type=F32
        )
    most = jnp.max(total, axis=1, keepdims=True)
    mark = jnp.where(most > MOST, float(MARK), 0.0)
    query = (low + high * float(LANES) + mark).astype(jnp.int32)
    for o in range(shards):
        queries[o] = query[o : o + 1, :]

    pl.semaphore_wait(barrier, shards - 1)
    exchange_rows(queries, asked, me, shards, gy_size, send_sem, recv_sem)
    own = pltpu.make_async_copy(queries.at[me], asked.at[me], own_sem)
    own.start()
    own.wait()
    await_rows(queries, asked, shards, gy_size, send_sem, recv_sem)
    top[...] = jnp.max(jnp.max(asked[...], axis=0), axis=1, keepdims=True)


def fetch_kernel(
    shards, gy_size, room, asked, table, landed, gramian,
    packed, wide, stage, outgoing, terms, arrived, row_total, table_sem, own_sem,
    send_sem, recv_sem, term_send, term_recv, sum_send, sum_recv,
):
    me = place(gy_size)
    barrier = signal_all(me, shards, gy_size)
    rows_dev = table.shape[0]
    parts = 8
    part = rows_dev // parts

    def load(c):
        rows = pl.ds(c * part, part)
        return pltpu.make_async_copy(table.at[rows], packed.at[rows], table_sem.at[c])

    for c in range(parts):
        load(c).start()
    piece = min(512, part)
    total = jnp.zeros((LANES, LANES), F32)
    for c in range(parts):
        load(c).wait()

        def step(j, total):
            rows = pl.ds(pl.multiple_of(c * part + j * piece, piece), piece)
            block = packed[rows, :]
            wide[rows, :] = block.astype(F32)
            return total + lax.dot_general(
                block, block, (((0,), (0,)), ((), ())), preferred_element_type=F32
            )

        total = lax.fori_loop(0, part // piece, step, total)
    for o in range(shards):
        terms[o] = total[o : o + 1, :]

    pl.semaphore_wait(barrier, shards - 1)
    exchange_rows(terms, arrived, me, shards, gy_size, term_send, term_recv)
    own_term = pltpu.make_async_copy(terms.at[me], arrived.at[me], own_sem.at[0])
    own_term.start()

    def collect(peer):
        for h in range(room // 16):
            for t in range(16):
                row = asked[peer, h * 16 + t] & (rows_dev - 1)
                stage[pl.ds(h * 16 + t, 1), :] = wide[pl.ds(row, 1), :]
        outgoing[peer] = stage[...].astype(BF16)

    def serve(i, carry):
        off = lax.rem(i * 77, shards)
        peer = lax.rem(me + off, shards)
        collect(peer)
        send(outgoing.at[peer], landed.at[me], send_sem, recv_sem, peer, gy_size).start()
        return carry

    lax.fori_loop(1, shards // 2, serve, 0)
    own_term.wait()
    await_rows(terms, arrived, shards, gy_size, term_send, term_recv)
    row_total[...] = jnp.sum(arrived[...], axis=0)

    def share(i, carry):
        peer = lax.rem(me + i, shards)
        send(row_total, gramian.at[me], sum_send, sum_recv, peer, gy_size).start()
        return carry

    lax.fori_loop(1, shards, share, 0)
    own_sum = pltpu.make_async_copy(row_total, gramian.at[me], own_sem.at[1])
    own_sum.start()
    lax.fori_loop(shards // 2, shards, serve, 0)
    collect(me)
    own = pltpu.make_async_copy(outgoing.at[me], landed.at[me], own_sem.at[2])
    own.start()
    own_sum.wait()
    own.wait()
    await_rows(terms, gramian, shards, gy_size, sum_send, sum_recv)
    await_rows(outgoing, landed, shards, gy_size, send_sem, recv_sem)


def bits(count):
    assert count & (count - 1) == 0
    return count.bit_length() - 1


def chip_of(device, gy_size):
    gx, gy = device // gy_size, lax.rem(device, gy_size)
    return (gx // CORES) * gy_size + gy, lax.rem(gx, CORES)


def shift_from(me, gy_size):
    gx, gy = me // gy_size, lax.rem(me, gy_size)
    y, core, x, z = gx // CORES, lax.rem(gx, CORES), gy // RING, lax.rem(gy, RING)

    def shifted(off):
        gx = lax.rem(y + off // (RING * RING * CORES), RING) * CORES
        gx = gx + lax.rem(core + off // (RING * RING), CORES)
        return gx, lax.rem(x + off // RING, RING) * RING + lax.rem(z + off, RING)

    return shifted


def conjugate(unobserved, gramian, confidence, counts, out, rows, vectors, weights):
    users = confidence.shape[1]
    unit = jnp.where(
        lax.broadcasted_iota(jnp.int32, (LANES, LANES), 0)
        == lax.broadcasted_iota(jnp.int32, (LANES, LANES), 1),
        1.0,
        0.0,
    ).astype(BF16)
    for item in range(USER_ITEMS):
        block = rows[pl.ds(item * users, users), :].astype(BF16)
        vectors[item] = lax.dot_general(
            unit, block, (((1,), (1,)), ((), ())), preferred_element_type=F32
        )

    item_sub = lax.broadcasted_iota(jnp.int32, (USER_ITEMS, users), 0)
    weights[...] = jnp.where(item_sub < counts[...], confidence[...], 0.0)
    scaled = gramian * unobserved
    top = scaled.astype(BF16)
    rest = (scaled - top.astype(F32)).astype(BF16)

    right = jnp.zeros((LANES, users), F32)
    for item in range(USER_ITEMS):
        right = right + vectors[item] * weights[item : item + 1, :]
    norm = jnp.sum(right * right, axis=0, keepdims=True)

    def sweep(_, carry):
        solution, residual, direction, norm = carry
        d_top = direction.astype(BF16)
        d_rest = (direction - d_top.astype(F32)).astype(BF16)
        image = direction
        unobserved_part = (
            jnp.dot(top, d_top, preferred_element_type=F32)
            + jnp.dot(top, d_rest, preferred_element_type=F32)
            + jnp.dot(rest, d_top, preferred_element_type=F32)
        )
        for item in range(USER_ITEMS):
            vector = vectors[item]
            projected = jnp.sum(vector * direction, axis=0, keepdims=True)
            image = image + vector * (weights[item : item + 1, :] * projected)
        image = image + unobserved_part
        alpha = norm / jnp.sum(direction * image, axis=0, keepdims=True)
        solution = solution + alpha * direction
        residual = residual - alpha * image
        after = jnp.sum(residual * residual, axis=0, keepdims=True)
        direction = residual + (after / norm) * direction
        return solution, residual, direction, after

    solution, *_ = lax.fori_loop(
        0, ITERATIONS, sweep, (jnp.zeros_like(right), right, right, norm)
    )
    out[...] = solution.T


def gather_kernel(
    shards, gy_size, blocks_dev, unobserved,
    ids, id_rows, owner_map, slots, offsets, counts, confidence, table, out, top,
    owners, found, queries, asked, asked_here, packed, twin_packed, wide, stage, outgoing,
    terms, arrived, row_total, spreads, starts, chips,
    landed, gramian, spots, spots_here, rows, vectors, weights, load_sem, own_sem, table_send, table_recv,
    send_sem, recv_sem, ask_send, ask_recv, term_send, term_recv, sum_send, sum_recv,
):
    me = place(gy_size)
    chip_me, core_me = chip_of(me, gy_size)
    barrier = signal_all(me, shards, gy_size)
    load_map = pltpu.make_async_copy(owner_map, owners, own_sem.at[0])
    load_map.start()
    rows_dev = table.shape[0]
    parts = 8
    part = rows_dev // parts

    def load(c):
        rows = pl.ds(c * part, part)
        return pltpu.make_async_copy(table.at[rows], packed.at[rows], load_sem.at[c])

    for c in range(parts):
        load(c).start()

    users = slots.shape[1]
    requests = found.shape[0]
    group = LANES // USER_BLOCKS
    lane = lax.broadcasted_iota(jnp.int32, (LANES, LANES), 1)
    sub = lax.broadcasted_iota(jnp.int32, (LANES, LANES), 0)
    lane_f = lane.astype(F32)
    diagonal = lane == sub

    item_sub = lax.broadcasted_iota(jnp.int32, (USER_ITEMS, users), 0)
    slot_lane = lax.broadcasted_iota(jnp.int32, (users, USER_ITEMS), 1)
    row_index = slots[...] * BLOCK + offsets[...]
    row_index = jnp.where(item_sub < counts[...], row_index, -1).astype(F32)
    inner = (id_rows[...] & (LANES - 1)).astype(F32)
    by_user = jnp.concatenate(
        [row_index, inner, jnp.zeros((LANES - USER_ITEMS - USER_BLOCKS, users), F32)], axis=0
    ).T
    row_index = by_user[:, :USER_ITEMS].astype(jnp.int32)
    inner = by_user.astype(BF16)
    wanted = lane == row_index[:, 0:1]
    for item in range(1, USER_ITEMS):
        wanted = wanted | (lane == row_index[:, item : item + 1])
    wanted = jnp.where(wanted, 1.0, 0.0).astype(BF16)
    wanted_inner = jnp.concatenate([wanted, inner], axis=1)

    load_map.wait()

    def look(user, carry):
        for slot in range(USER_BLOCKS):
            line = lax.shift_right_logical(ids[slot, user], bits(LANES))
            found[pl.ds(user * USER_BLOCKS + slot, 1), :] = owners[pl.ds(line, 1), :]
        return carry

    lax.fori_loop(0, users, look, 0, unroll=2)

    same = lax.shift_right_logical(lane, 3) == (sub & 7)
    own_lane = lane == (sub & 7) + USER_ITEMS
    earlier = jnp.where(lane < sub, 1.0, 0.0).astype(BF16)
    before_row = jnp.where(
        (lax.shift_right_logical(lane, 3) == lax.shift_right_logical(sub, 3))
        & ((sub & 7) < (lane & 7)),
        1.0,
        0.0,
    ).astype(BF16)
    up_to = jnp.concatenate(
        [jnp.where((sub & 7) <= r, 1.0, 0.0).astype(BF16) for r in range(BLOCK)], axis=1
    )
    total = jnp.zeros((1, LANES), F32)
    low_high = jnp.zeros((LANES, 2 * LANES), F32)
    for a in range(requests // LANES):
        pick = jnp.where(lax.shift_right_logical(sub, bits(USER_BLOCKS)) + a * group == lane, 1.0, 0.0).astype(BF16)
        picked = jnp.dot(pick, wanted_inner, preferred_element_type=F32)
        spread = jnp.where(same, picked[:, :LANES], 0.0).astype(BF16)
        inner_here = jnp.sum(jnp.where(own_lane, picked[:, LANES:], 0.0), axis=1, keepdims=True)
        line = found[pl.ds(a * LANES, LANES), :].astype(F32)
        storage = jnp.sum(jnp.where(lane_f == inner_here, line, 0.0), axis=1, keepdims=True)
        storage = storage.astype(jnp.int32)
        device = lax.shift_right_logical(storage, bits(blocks_dev))
        within = storage & (blocks_dev - 1)
        gx = lax.shift_right_logical(device, bits(gy_size))
        chip = lax.shift_right_logical(gx, bits(CORES)) * gy_size + (device & (gy_size - 1))
        core = gx & (CORES - 1)
        low_first = ((within & 15) * BLOCK).astype(F32)
        high = (core * (rows_dev // LANES) + lax.shift_right_logical(within, 4)).astype(F32)
        chip = chip.astype(F32)
        so_far = jnp.dot(spread, up_to, preferred_element_type=F32)
        so_far = [so_far[:, r * LANES : (r + 1) * LANES] for r in range(BLOCK)]
        mine = lane_f == chip
        counted = jnp.where(mine, so_far[-1], 0.0)
        before = jnp.dot(earlier, counted.astype(BF16), preferred_element_type=F32) + total
        start = jnp.sum(jnp.where(mine, before, 0.0), axis=1, keepdims=True)
        total = total + jnp.sum(counted, axis=0, keepdims=True)
        depth = lane_f - start
        which = jnp.zeros((LANES, LANES), F32)
        for m in so_far:
            which = which + jnp.where(m <= depth, 1.0, 0.0)
        hit = (depth >= 0.0) & (depth < so_far[-1])
        both = jnp.concatenate(
            [jnp.where(hit, low_first + which, 0.0), jnp.where(hit, high, 0.0)], axis=1
        ).astype(BF16)
        chip_row = jnp.sum(jnp.where(diagonal, chip, 0.0), axis=0, keepdims=True)
        to_chip = jnp.where(sub.astype(F32) == chip_row, 1.0, 0.0).astype(BF16)
        low_high = low_high + jnp.dot(to_chip, both, preferred_element_type=F32)
        here = pl.ds(a * LANES, LANES)
        spreads[here, :] = spread
        starts[here, :] = jnp.broadcast_to(start, (LANES, LANES))
        chips[here, :] = jnp.broadcast_to(chip, (LANES, LANES))
    most = jnp.max(total, axis=1, keepdims=True)
    mark = jnp.where(most > CHIP_ROOM, float(MARK), 0.0)
    query = (low_high[:, :LANES] + low_high[:, LANES:] * float(LANES) + mark).astype(jnp.int32)
    for core in range(CORES):
        shares = pltpu.roll(query, LANES - core * ROOM, 1) if core else query
        for o in range(shards // CORES):
            device = (o // gy_size * CORES + core) * gy_size + o % gy_size
            queries[device] = shares[o : o + 1, :]

    piece = min(512, rows_dev)
    mine_from = core_me * rows_dev
    theirs_from = (CORES - 1 - core_me) * rows_dev

    def widen(source, start, j, carry):
        at = j * piece
        block = source[pl.ds(pl.multiple_of(at, piece), piece), :]
        wide[pl.ds(pl.multiple_of(start + at, piece), piece), :] = block.astype(F32)
        return carry

    for c in range(parts):
        load(c).wait()
    lax.fori_loop(0, rows_dev // piece, functools.partial(widen, packed, mine_from), 0)

    pl.semaphore_wait(barrier, shards - 1)
    shifted = shift_from(me, gy_size)
    twin = shifted(RING * RING)
    lend = send(table, twin_packed, table_send, table_recv, twin, gy_size)
    exchange_rows(queries, asked, me, shards, gy_size, ask_send, ask_recv)
    lend.start()
    own_ask = pltpu.make_async_copy(queries.at[me], asked.at[me], own_sem.at[1])
    own_ask.start()

    slab = min(2048, rows_dev)

    def step(j, gram):
        block = packed[pl.ds(pl.multiple_of(j * slab, slab), slab), :]
        return gram + lax.dot_general(
            block, block, (((0,), (0,)), ((), ())), preferred_element_type=F32
        )

    gram = lax.fori_loop(0, rows_dev // slab, step, jnp.zeros((LANES, LANES), F32))
    for o in range(LANES):
        terms[o] = gram[o : o + 1, :]
    exchange_rows(terms, arrived, me, shards, gy_size, term_send, term_recv)
    own_term = pltpu.make_async_copy(terms.at[me], arrived.at[me], own_sem.at[2])
    own_term.start()

    own_ask.wait()
    await_rows(asked, asked, shards, gy_size, ask_send, ask_recv)
    to_scalars = pltpu.make_async_copy(asked, asked_here, own_sem.at[3])
    to_scalars.start()
    lend.wait()
    lax.fori_loop(0, rows_dev // piece, functools.partial(widen, twin_packed, theirs_from), 0)
    to_scalars.wait()

    my_place = chip_me * CORES + core_me

    def collect(peer):
        for t in range(ROOM):
            row = asked_here[peer, 0, t] & (CORES * rows_dev - 1)
            stage[pl.ds(t, 1), :] = wide[pl.ds(row, 1), :]
        outgoing[peer] = stage[...].astype(BF16)

    def serve(i, carry):
        gx, gy = shifted(lax.rem(i * (77 - 26 * core_me), shards))
        peer = gx * gy_size + gy
        collect(peer)
        send(outgoing.at[peer], landed.at[my_place], send_sem, recv_sem, (gx, gy), gy_size).start()
        return carry

    lax.fori_loop(1, SECOND, serve, 0)
    own_term.wait()
    await_rows(terms, arrived, shards, gy_size, term_send, term_recv)
    row_total[...] = jnp.sum(arrived[...], axis=0)

    def share(i, carry):
        peer = lax.rem(me + i, shards)
        send(row_total, gramian.at[me], sum_send, sum_recv, peer, gy_size).start()
        return carry

    lax.fori_loop(1, shards, share, 0)
    own_sum = pltpu.make_async_copy(row_total, gramian.at[me], own_sem.at[4])
    own_sum.start()
    lax.fori_loop(SECOND, shards, serve, 0)
    collect(me)
    own = pltpu.make_async_copy(outgoing.at[me], landed.at[my_place], own_sem.at[5])
    own.start()

    pos_chip = jnp.zeros((users, 2 * LANES), F32)
    for a in range(requests // LANES):
        here = pl.ds(a * LANES, LANES)
        back = lax.shift_right_logical(lane, bits(USER_BLOCKS)) + a * group == sub
        spread = spreads[here, :]
        live = spread.astype(F32) > 0.0
        spot = jnp.dot(spread, before_row, preferred_element_type=F32) + starts[here, :]
        both = jnp.concatenate(
            [jnp.where(live, spot, 0.0), jnp.where(live, chips[here, :], 0.0)], axis=1
        ).astype(BF16)
        back = jnp.where(back, 1.0, 0.0).astype(BF16)
        pos_chip = pos_chip + jnp.dot(back, both, preferred_element_type=F32)
    spot = pos_chip[:, :LANES] + pos_chip[:, LANES:] * float(CHIP_ROOM)
    spots_now = jnp.zeros((users, USER_ITEMS), F32)
    for item in range(USER_ITEMS):
        chosen = jnp.where(lane == row_index[:, item : item + 1], spot, 0.0)
        chosen = jnp.sum(chosen, axis=1, keepdims=True)
        spots_now = jnp.where(slot_lane == item, chosen, spots_now)
    spots[...] = spots_now.astype(jnp.int32) & (CORES * rows_dev - 1)
    top[...] = jnp.max(jnp.max(asked[...], axis=0), axis=1, keepdims=True)

    spots_to = pltpu.make_async_copy(spots, spots_here, own_sem.at[0])
    spots_to.start()

    own_sum.wait()
    own.wait()
    await_rows(terms, gramian, shards, gy_size, sum_send, sum_recv)
    spots_to.wait()
    await_rows(outgoing, landed, shards, gy_size, send_sem, recv_sem)

    def widen_landed(j, carry):
        for t in range(8):
            at = pl.ds(pl.multiple_of((j * 8 + t) * ROOM, ROOM), ROOM)
            wide[at, :] = landed[j * 8 + t].astype(F32)
        return carry

    lax.fori_loop(0, shards // 8, widen_landed, 0)

    def take(user, carry):
        for item in range(USER_ITEMS):
            rows[pl.ds(item * users + user, 1), :] = wide[pl.ds(spots_here[user, item], 1), :]
        return carry

    lax.fori_loop(0, users, take, 0)
    whole = jnp.concatenate([gramian[o] for o in range(LANES)], axis=0)
    conjugate(unobserved, whole, confidence, counts, out, rows, vectors, weights)


def solve_kernel(
    unobserved, spots, landed, gramian, confidence, counts, out, packed, wide, rows, vectors, weights, sem
):
    users = confidence.shape[1]
    parts = 8
    part = landed.shape[0] // parts

    def load(c):
        here = pl.ds(c * part, part)
        return pltpu.make_async_copy(landed.at[here], packed.at[here], sem.at[c])

    for c in range(parts):
        load(c).start()
    for c in range(parts):
        load(c).wait()
        here = pl.ds(c * part, part)
        wide[here, :] = packed[here, :].astype(F32)

    def pick(user, carry):
        for item in range(USER_ITEMS):
            rows[pl.ds(item * users + user, 1), :] = wide[pl.ds(spots[user, item], 1), :]
        return carry

    lax.fori_loop(0, users, pick, 0)
    conjugate(unobserved, gramian[...], confidence, counts, out, rows, vectors, weights)


def vmem():
    return pl.BlockSpec(memory_space=pltpu.VMEM)


def smem():
    return pl.BlockSpec(memory_space=pltpu.SMEM)


def anywhere():
    return pl.BlockSpec(memory_space=pl.ANY)


def ask(shards, gy_size, blocks_dev, ids, owner_map, need):
    requests = need.shape[0]
    dma = pltpu.SemaphoreType.DMA
    return pl.pallas_call(
        functools.partial(ask_kernel, shards, gy_size, blocks_dev),
        out_shape=(
            jax.ShapeDtypeStruct((shards, 1, LANES), jnp.int32),
            jax.ShapeDtypeStruct((requests, BLOCK), jnp.int32),
            jax.ShapeDtypeStruct((1, 1), jnp.int32),
        ),
        in_specs=[smem(), anywhere(), vmem()],
        out_specs=(vmem(), vmem(), vmem()),
        scratch_shapes=[
            pltpu.VMEM(owner_map.shape, jnp.int32),
            pltpu.VMEM((requests, LANES), jnp.int32),
            pltpu.VMEM((shards, 1, LANES), jnp.int32),
            dma, dma, dma, dma,
        ],
        compiler_params=pltpu.CompilerParams(
            collective_id=1, has_side_effects=True, vmem_limit_bytes=VMEM_LIMIT
        ),
        name="ask",
    )(ids, owner_map, need)


def fetch(shards, gy_size, room, asked, table):
    dma = pltpu.SemaphoreType.DMA
    return pl.pallas_call(
        functools.partial(fetch_kernel, shards, gy_size, room),
        out_shape=(
            jax.ShapeDtypeStruct((shards, room, LANES), BF16),
            jax.ShapeDtypeStruct((shards, 1, LANES), F32),
        ),
        in_specs=[smem(), anywhere()],
        out_specs=(anywhere(), vmem()),
        scratch_shapes=[
            pltpu.VMEM(table.shape, BF16),
            pltpu.VMEM(table.shape, F32),
            pltpu.VMEM((room, LANES), F32),
            pltpu.VMEM((shards, room, LANES), BF16),
            pltpu.VMEM((shards, 1, LANES), F32),
            pltpu.VMEM((shards, 1, LANES), F32),
            pltpu.VMEM((1, LANES), F32),
            pltpu.SemaphoreType.DMA((8,)),
            pltpu.SemaphoreType.DMA((3,)),
            dma, dma, dma, dma, dma, dma,
        ],
        compiler_params=pltpu.CompilerParams(
            collective_id=2,
            has_side_effects=True,
            vmem_limit_bytes=VMEM_LIMIT,
        ),
        name="fetch",
    )(asked, table)


def gather(
    shards, gy_size, blocks_dev, unobserved, block_ids, owner_map, slots, offsets, counts, confidence, table
):
    dma = pltpu.SemaphoreType.DMA
    users = slots.shape[1]
    line = (shards, 1, LANES)
    return pl.pallas_call(
        functools.partial(gather_kernel, shards, gy_size, blocks_dev, unobserved),
        out_shape=(
            jax.ShapeDtypeStruct((users, LANES), F32),
            jax.ShapeDtypeStruct((1, 1), jnp.int32),
        ),
        in_specs=[smem(), vmem(), anywhere(), vmem(), vmem(), vmem(), vmem(), anywhere()],
        out_specs=(vmem(), vmem()),
        scratch_shapes=[
            pltpu.VMEM(owner_map.shape, jnp.int32),
            pltpu.VMEM((users * USER_BLOCKS, LANES), jnp.int32),
            pltpu.VMEM(line, jnp.int32),
            pltpu.VMEM(line, jnp.int32),
            pltpu.SMEM(line, jnp.int32),
            pltpu.VMEM(table.shape, BF16),
            pltpu.VMEM(table.shape, BF16),
            pltpu.VMEM((CORES * table.shape[0], LANES), F32),
            pltpu.VMEM((ROOM, LANES), F32),
            pltpu.VMEM((shards, ROOM, LANES), BF16),
            pltpu.VMEM(line, F32),
            pltpu.VMEM(line, F32),
            pltpu.VMEM((1, LANES), F32),
            pltpu.VMEM((users * USER_BLOCKS, LANES), BF16),
            pltpu.VMEM((users * USER_BLOCKS, LANES), F32),
            pltpu.VMEM((users * USER_BLOCKS, LANES), F32),
            pltpu.VMEM((shards, ROOM, LANES), BF16),
            pltpu.VMEM(line, F32),
            pltpu.VMEM((users, USER_ITEMS), jnp.int32),
            pltpu.SMEM((users, USER_ITEMS), jnp.int32),
            pltpu.VMEM((USER_ITEMS * users, LANES), F32),
            pltpu.VMEM((USER_ITEMS, LANES, users), F32),
            pltpu.VMEM((USER_ITEMS, users), F32),
            pltpu.SemaphoreType.DMA((8,)),
            pltpu.SemaphoreType.DMA((6,)),
            dma, dma, dma, dma, dma, dma, dma, dma, dma, dma,
        ],
        compiler_params=pltpu.CompilerParams(
            collective_id=0, has_side_effects=True, vmem_limit_bytes=VMEM_LIMIT
        ),
        name="gather",
    )(block_ids, block_ids, owner_map, slots, offsets, counts, confidence, table)


def solve(unobserved, spots, landed, gramian, confidence, counts):
    users = confidence.shape[1]
    return pl.pallas_call(
        functools.partial(solve_kernel, unobserved),
        out_shape=jax.ShapeDtypeStruct((users, LANES), F32),
        in_specs=[smem(), anywhere(), vmem(), vmem(), vmem()],
        out_specs=vmem(),
        scratch_shapes=[
            pltpu.VMEM(landed.shape, BF16),
            pltpu.VMEM(landed.shape, F32),
            pltpu.VMEM((USER_ITEMS * users, LANES), F32),
            pltpu.VMEM((USER_ITEMS, LANES, users), F32),
            pltpu.VMEM((USER_ITEMS, users), F32),
            pltpu.SemaphoreType.DMA((8,)),
        ],
        compiler_params=pltpu.CompilerParams(vmem_limit_bytes=VMEM_LIMIT),
        name="solve",
    )(spots, landed, gramian, confidence, counts)


def fetch_all(shards, gy_size, blocks_dev, item_table, block_ids, item_slots, item_offsets, item_counts, owner_map):
    users = block_ids.shape[0]
    live = jnp.arange(USER_ITEMS)[None, :] < item_counts[:, None]
    row_index = item_slots * BLOCK + item_offsets
    candidates = jnp.arange(USER_BLOCKS * BLOCK, dtype=jnp.int32)
    hits = row_index[:, :, None] == candidates[None, None, :]
    need = jnp.any(hits & live[:, :, None], axis=1).astype(F32)
    asked, keys, _ = ask(
        shards,
        gy_size,
        blocks_dev,
        block_ids.reshape(-1, LANES),
        owner_map,
        need.reshape(users * USER_BLOCKS, BLOCK),
    )
    keys = keys.reshape(users, 1, USER_BLOCKS * BLOCK)
    spots = jnp.sum(jnp.where(hits, keys, 0), axis=2)
    landed, gramian = fetch(shards, gy_size, MOST, asked.reshape(shards, LANES), item_table)
    return spots, landed, gramian


def per_device(item_table, block_ids, item_slots, item_offsets, confidence, item_counts, owner_map):
    shards, gy_size = lax.axis_size(("gx", "gy")), lax.axis_size("gy")
    rows_dev = item_table.shape[0]
    blocks_dev = rows_dev // BLOCK
    users = block_ids.shape[0]
    unobserved = USER_ITEMS / (rows_dev * shards)
    owner_map = owner_map.reshape(-1, LANES)
    counts = item_counts.reshape(1, users)

    def finish(spots, landed, gramian):
        landed = landed.reshape(-1, LANES)
        gramian = gramian.reshape(LANES, LANES)
        return solve(unobserved, spots, landed, gramian, confidence.T, counts)

    factors, top = gather(
        shards, gy_size, blocks_dev, unobserved, block_ids.T, owner_map,
        item_slots.T, item_offsets.T, counts, confidence.T, item_table,
    )
    return lax.cond(
        top[0, 0] >= MARK,
        lambda: finish(
            *fetch_all(
                shards, gy_size, blocks_dev, item_table, block_ids,
                item_slots, item_offsets, item_counts, owner_map,
            )
        ),
        lambda: factors,
    )


def solution(mesh):
    return jax.shard_map(
        per_device,
        mesh=mesh,
        in_specs=(
            P(("gx", "gy"), None),
            P(("gx", "gy"), None),
            P(("gx", "gy"), None),
            P(("gx", "gy"), None),
            P(("gx", "gy"), None),
            P(("gx", "gy")),
            P(),
        ),
        out_specs=P(("gx", "gy"), None),
        check_vma=False,
    )
```
